256 devices in a mesh: dp: 16 (over z, y_hi), mp: 16 (over y_lo, x, core).
Axes of the slice: x: 4, y: 4 (y_hi: 2, y_lo: 2; y = y_hi * 2 + y_lo), z: 8, core: 2. Of those that a mesh axis runs over, the one named last changes fastest.
Arguments:
- activations: bfloat16 [2048, 4096], P('dp', 'mp'), may hold values from -6 to 6
- out_grad: bfloat16 [2048, 16384], P('dp', 'mp'), may hold values from -0.125 to 0.125
- block_slot: int32 [16, 16], replicated, may hold values from 0 to 15, each once within a row
- refresh_list: int32 [16, 4], replicated, may hold values from 0 to 15, as said below
- left_factor: float32 [16, 16, 512, 512], P('dp', 'mp'), as said below
- right_factor: float32 [16, 16, 512, 512], P('dp', 'mp'), as said below
- left_root: bfloat16 [16, 16, 512, 512], P('dp', 'mp'), as said below
- right_root: bfloat16 [16, 16, 512, 512], P('dp', 'mp'), as said below
Outputs:
- direction: bfloat16 [4096, 16384], P(None, 'mp')
- new_left_root: bfloat16 [16, 16, 512, 512], P('dp', 'mp')
- new_right_root: bfloat16 [16, 16, 512, 512], P('dp', 'mp')
The draws below stay inside these ranges and needn't reach their ends.
Inputs may be any that keep to these rules, and one draw needn't show every extreme that they name: `block_slot`: each row is a permutation of the 16 slots; slot s of a strip belongs to dp index s. `refresh_list`: each row names 4 different blocks of its strip. `left_factor`: every tile is symmetric, with a positive diagonal that exceeds the sum of the magnitudes of its row's other entries. `right_factor`: every tile is symmetric, with a positive diagonal that exceeds the sum of the magnitudes of its row's other entries. `left_root`: every tile is symmetric. `right_root`: every tile is symmetric.
All inputs are finite; a program needn't handle non-finite values.
Results may differ from the reference program's by a relative error of at most 0.0064.
Values may be sent and summed in bfloat16 or wider, within the bound.
A program may use at most 128 MiB of HBM per device.

```python
import jax
import jax.numpy as jnp
from jax import lax

D = 4096
FFW = 16384
B = 512
ITERS = 3
REFRESH = 4
TOKENS = 2048
STRIPS = 16
STRIP = 1024
NBG = 16


def dominant_tiles(key, low, high, spread):
    first, second = jax.random.split(key)
    diagonal = low * jnp.exp(jax.random.uniform(first, (NBG, STRIPS, B), jnp.float32) * jnp.log(high / low))
    noise = jax.random.uniform(second, (NBG, STRIPS, B, B), jnp.float32, -1.0, 1.0)
    symmetric = (noise + jnp.swapaxes(noise, -1, -2)) * 0.5 * spread / B
    identity = jnp.eye(B, dtype=jnp.float32)
    return symmetric * (1.0 - identity) + diagonal[..., :, None] * identity


def draw_refresh_list(key, part):
    key = jax.random.fold_in(key, 7)
    keys = jax.random.split(key, STRIPS)
    perms = jax.vmap(lambda one: jax.random.permutation(one, NBG))(keys).astype(jnp.int32)
    shift = jnp.zeros((STRIPS,), jnp.int32).at[0].set(NBG - 1 - perms[0, 0]).at[1].set(-perms[1, 0])
    rows = (perms + shift[:, None]) % NBG
    return rows[:, :REFRESH]


def draw_left_factor(key, part):
    key = jax.random.fold_in(key, 11)
    tiles = dominant_tiles(key, 1.0, 4.0, 0.7) * (B * 0.5)
    return tiles


def draw_right_factor(key, part):
    key = jax.random.fold_in(key, 13)
    tiles = dominant_tiles(key, 1.0, 4.0, 0.7) * (B * 0.5)
    return tiles


def draw_left_root(key, part):
    key = jax.random.fold_in(key, 17)
    tiles = dominant_tiles(key, 0.15, 0.4, 0.6)
    return tiles.astype(jnp.bfloat16)


def draw_right_root(key, part):
    key = jax.random.fold_in(key, 19)
    tiles = dominant_tiles(key, 0.15, 0.4, 0.6)
    return tiles.astype(jnp.bfloat16)


def steps_of(own_key, dims, cuts, least, high):
    gain, own = 1.0, jax.random.fold_in(own_key, 6)
    for dim, parts in cuts:
        steps = jnp.exp(jax.random.uniform(jax.random.fold_in(own, dim), (parts,), jnp.float32, least / len(cuts), high / len(cuts)))
        gain = gain * jnp.repeat(steps, dims[dim] // parts).reshape([-1 if axis == dim else 1 for axis in range(len(dims))])
    return gain


def normal_values(rng, extent, deviation, bound, pieces=(), held_as=jnp.bfloat16):
    drawn = deviation * jax.random.normal(rng, extent, jnp.float32)
    if pieces:
        drawn = drawn * steps_of(rng, extent, pieces, -0.22, 0.18)
    return jnp.clip(drawn, -bound, bound).astype(held_as)


def setup_inputs(seed: int = 0) -> dict:
    splits = jax.random.split(jax.random.key(seed), 9)
    return {
        "activations": normal_values(splits[0], (TOKENS, D), 1.0, 6.0, ((0, 16), (1, 16))),
        "out_grad": normal_values(splits[1], (TOKENS, FFW), TOKENS ** -0.5, 0.125, ((0, 16), (1, 16))),
        "block_slot": jax.vmap(lambda own: jax.random.permutation(own, NBG))(jax.random.split(splits[2], STRIPS)).reshape((STRIPS, NBG)).astype(jnp.int32),
        "refresh_list": draw_refresh_list(jax.random.fold_in(splits[8], 71), 0),
        "left_factor": draw_left_factor(jax.random.fold_in(splits[8], 71), 0),
        "right_factor": draw_right_factor(jax.random.fold_in(splits[8], 71), 0),
        "left_root": draw_left_root(jax.random.fold_in(splits[8], 71), 0),
        "right_root": draw_right_root(jax.random.fold_in(splits[8], 71), 0),
    }


def matmul(left, right):
    return jnp.dot(left.astype(jnp.float32), right.astype(jnp.float32), precision=lax.Precision.HIGHEST)

def inverse_root(statistic):
    size = statistic.shape[-1]
    identity = jnp.eye(size, dtype=jnp.float32)
    scaling = 2.5 / jnp.sqrt(jnp.sum(statistic * statistic))
    iterate = identity * scaling ** 0.25
    powered = statistic * scaling
    for step in range(ITERS):
        factor = (5.0 * identity - powered) * 0.25
        iterate = matmul(iterate, factor)
        square = matmul(factor, factor)
        fourth = matmul(square, square)
        powered = matmul(fourth, powered)
    return iterate.astype(jnp.bfloat16)

def reference(activations, out_grad, block_slot, refresh_list, left_factor, right_factor, left_root, right_root):
    act_full = activations.astype(jnp.float32)
    col_blocks = STRIP // B
    high = lax.Precision.HIGHEST

    def one_strip(strip_id):
        columns = lax.dynamic_slice_in_dim(out_grad, strip_id * STRIP, STRIP, 1).astype(jnp.float32)
        gradient = jnp.dot(act_full.T, columns, precision=high).astype(jnp.bfloat16)
        tiles = gradient.reshape(D // B, B, col_blocks, B).transpose(0, 2, 1, 3).reshape(NBG, B, B)
        slots = block_slot[strip_id]
        tiles_f = tiles.astype(jnp.float32)
        left_stat = 0.9 * left_factor[:, strip_id][slots] + jnp.einsum('nab,ncb->nac', tiles_f, tiles_f, precision=high)
        right_stat = 0.9 * right_factor[:, strip_id][slots] + jnp.einsum('nba,nbc->nac', tiles_f, tiles_f, precision=high)
        picks = refresh_list[strip_id]
        left_now = left_root[:, strip_id][slots]
        right_now = right_root[:, strip_id][slots]
        left_now = left_now.at[picks].set(lax.map(inverse_root, left_stat[picks]))
        right_now = right_now.at[picks].set(lax.map(inverse_root, right_stat[picks]))
        mixed = jnp.einsum('nab,nbc->nac', left_now.astype(jnp.float32), tiles_f, precision=high).astype(jnp.bfloat16)
        precond = jnp.einsum('nab,nbc->nac', mixed.astype(jnp.float32), right_now.astype(jnp.float32), precision=high)
        grad_sq = lax.optimization_barrier(jnp.sum(tiles_f * tiles_f, axis=(1, 2)))
        pre_sq = lax.optimization_barrier(jnp.sum(precond * precond, axis=(1, 2)))
        ratio = jnp.sqrt((grad_sq + 1e-06) / (pre_sq + 1e-06))
        tiles_out = (precond * ratio[:, None, None]).astype(jnp.bfloat16)
        strip_out = tiles_out.reshape(D // B, col_blocks, B, B).transpose(0, 2, 1, 3).reshape(D, STRIP)
        left_slots = jnp.zeros_like(left_now).at[slots].set(left_now)
        right_slots = jnp.zeros_like(right_now).at[slots].set(right_now)
        return (strip_out, left_slots, right_slots)
    strips_out, left_all, right_all = lax.map(one_strip, jnp.arange(STRIPS, dtype=jnp.int32))
    direction = strips_out.transpose(1, 0, 2).reshape(D, FFW)
    return (direction, jnp.swapaxes(left_all, 0, 1), jnp.swapaxes(right_all, 0, 1))
```

```python
import functools

import jax
import jax.numpy as jnp
from jax import lax
from jax.experimental import pallas as pl
from jax.experimental.pallas import tpu as pltpu
from jax.sharding import PartitionSpec as P

NZ, NX, NY = 8, 4, 4
SIDE = 512
FEAT = 64
A_ROWS = 288
HALF = A_ROWS // 2
MESH = pl.DeviceIdType.MESH
VMEM_LIMIT = 48 * 1024 * 1024


def place():
    dp, mp = lax.axis_index("dp"), lax.axis_index("mp")
    return dp // 2, dp % 2, mp // 8, (mp // 2) % 4, mp % 2


def device(z, h, l, x, k):
    return (2 * z + h, 8 * l + 2 * x + k)


def gradient_kernel(
    slots_ref, act_ref, out_ref, grad_ref,
    cot, act, flipped, total, pieces, outgoing, tile,
    swap_s, swap_r, ring_s, ring_r, turn_s, turn_r, plane_s, plane_r,
    pass_s, pass_r, give_s, give_r, local_s,
):
    z, h, l, x, k = place()
    dp, mp = lax.axis_index("dp"), lax.axis_index("mp")
    y = 2 * h + l
    r = 4 * l + x
    up, down = (z + 1) % NZ, (z + NZ - 1) % NZ

    barrier = pltpu.get_barrier_semaphore()

    def greet(target):
        pl.semaphore_signal(barrier, inc=1, device_id=target, device_id_type=MESH)

    for step in range(1, 16):
        greet(((dp + step) % 16, mp))
    for dy in range(NY):
        for dx in range(NX):
            if (dy, dx) != (0, 0):
                ty, tx = (y + dy) % NY, (x + dx) % NX
                greet(device(z, ty // 2, ty % 2, tx, k))
    for step in range(NZ):
        greet(device((z + step) % NZ, h, l, x, 1 - k))

    for c in range(2):
        cot[z, pl.ds(h * 128, 128), c * 256 : c * 256 + 256] = out_ref[
            :, pl.ds(pl.multiple_of(c * 512 + 256 * h, 256), 256)
        ]
    flipped[...] = act_ref[...].astype(jnp.float32).T.astype(jnp.bfloat16)
    pl.semaphore_wait(barrier, 38)

    def send(src, dst, ssem, rsem, target):
        copy = pltpu.make_async_remote_copy(
            src_ref=src, dst_ref=dst, send_sem=ssem, recv_sem=rsem, device_id=target, device_id_type=MESH
        )
        copy.start()
        return copy

    pending = []

    def turn_view(source):
        return act.at[source // 2, source % 2, r, :, pl.ds(pl.multiple_of(h * 128, 128), 128)]

    for j in range(4):
        target = 4 * k + j
        here = jnp.logical_and(target == z, z % 2 == k)
        src = flipped.at[j * FEAT : (j + 1) * FEAT, :]

        @pl.when(jnp.logical_not(here))
        def _():
            send(src, turn_view(z), turn_s.at[j], turn_r.at[z], device(target, h, l, x, z % 2))

        @pl.when(here)
        def _():
            pltpu.make_async_copy(src, turn_view(z), turn_r.at[z]).start()

    for c in range(2):
        pending.append(
            send(
                out_ref.at[:, pl.ds(pl.multiple_of(c * 512 + 256 * (1 - h), 256), 256)],
                cot.at[z, pl.ds(pl.multiple_of(h * 128, 128), 128), pl.ds(c * 256, 256)],
                swap_s.at[c], swap_r.at[c], (2 * z + 1 - h, mp),
            )
        )

    def unit(source, u):
        return cot.at[source, pl.ds(pl.multiple_of(u * 128, 128), 128), :]

    def ring(direction, step, u):
        source = (z + NZ - step) % NZ if direction == 0 else (z + step) % NZ
        target = up if direction == 0 else down
        view = unit(source, u)
        pending.append(
            send(view, view, ring_s.at[direction, step, u], ring_r.at[direction, step, u], (2 * target + h, mp))
        )

    def ring_wait(direction, step, u):
        source = (z + NZ - step) % NZ if direction == 0 else (z + step) % NZ
        view = unit(source, u)
        pltpu.make_async_remote_copy(
            src_ref=view, dst_ref=view, send_sem=ring_s.at[direction, step - 1, u],
            recv_sem=ring_r.at[direction, step - 1, u], device_id=(dp, mp), device_id_type=MESH,
        ).wait_recv()

    ring(0, 0, h)
    ring(1, 0, h)

    for i in range(4):
        source = 2 * i + k
        view = turn_view(source)
        pltpu.make_async_copy(view, view, turn_r.at[source]).wait()

    def plane_view(row, half):
        return act.at[:, k, row, :, pl.ds(pl.multiple_of(half * 128, 128), 128)]

    for dy in range(NY):
        for dx in range(NX):
            if (dy, dx) != (0, 0):
                ty, tx = (y + dy) % NY, (x + dx) % NX
                view = plane_view(r, h)
                pending.append(
                    send(view, view, plane_s.at[4 * dy + dx], plane_r.at[4 * dy + dx], device(z, ty // 2, ty % 2, tx, k))
                )

    for c in range(2):
        view = cot.at[z, pl.ds(pl.multiple_of((1 - h) * 128, 128), 128), pl.ds(c * 256, 256)]
        pltpu.make_async_copy(view, view, swap_r.at[c]).wait()
    ring(0, 0, 1 - h)
    ring(1, 0, 1 - h)

    for step in (1, 2):
        for u in (h, 1 - h):
            for direction in (0, 1):
                ring_wait(direction, step, u)
                ring(direction, step, u)

    for dy in range(NY):
        for dx in range(NX):
            if (dy, dx) != (0, 0):
                sy, sx = (y + NY - dy) % NY, (x + NX - dx) % NX
                view = plane_view(4 * (sy % 2) + sx, sy // 2)
                pltpu.make_async_copy(view, view, plane_r.at[4 * dy + dx]).wait()
    for row in range(8):
        view = act.at[:, k, row]
        pending.append(send(view, view, pass_s.at[row], pass_r.at[row], device(z, h, l, x, 1 - k)))

    for u in (h, 1 - h):
        for direction in (0, 1):
            ring_wait(direction, 3, u)
    ring(0, 3, 0)
    ring(1, 3, 1)

    for row in range(8):
        view = act.at[:, 1 - k, row]
        pltpu.make_async_copy(view, view, pass_r.at[row]).wait()

    def product(source):
        return jnp.dot(
            act[source // 2, source % 2].reshape(8 * FEAT, 256), cot[source], preferred_element_type=jnp.float32
        )

    total[...] = product(z)

    @pl.loop(1, 4)
    def _(step):
        total[...] += product((z + step) % NZ)
        total[...] += product((z + NZ - step) % NZ)

    ring_wait(0, 4, 0)
    ring_wait(1, 4, 1)
    total[...] += product((z + 4) % NZ)

    for row in range(8):
        for c in range(2):
            pieces[2 * row + c] = total[row * FEAT : (row + 1) * FEAT, c * 256 : (c + 1) * 256].astype(jnp.bfloat16)

    def spot(slot):
        return tile.at[
            pl.ds(pl.multiple_of((slot // 2) * FEAT, FEAT), FEAT), pl.ds(pl.multiple_of((slot % 2) * 256, 256), 256)
        ]

    def held(slot):
        found = jnp.int32(0)
        for b in range(16):
            found = jnp.maximum(found, jnp.where(slots_ref[mp, b] == slot, b, 0))
        return found

    @pl.loop(1, 16)
    def _(step):
        slot = (dp + step) % 16
        outgoing[slot] = pieces[held(slot)]
        send(outgoing.at[slot], spot(dp), give_s.at[slot], give_r.at[dp], (slot, mp))

    outgoing[dp] = pieces[held(dp)]
    own = pltpu.make_async_copy(outgoing.at[dp], spot(dp), local_s)
    own.start()
    own.wait()

    @pl.loop(1, 16)
    def _(step):
        slot = (dp + step) % 16
        view = spot(slot)
        pltpu.make_async_copy(view, view, give_r.at[slot]).wait()
        pltpu.make_async_copy(outgoing.at[slot], outgoing.at[slot], give_s.at[slot]).wait()

    for copy in pending:
        copy.wait_send()
    for j in range(4):
        here = jnp.logical_and(4 * k + j == z, z % 2 == k)
        src = flipped.at[j * FEAT : (j + 1) * FEAT, :]

        @pl.when(jnp.logical_not(here))
        def _():
            pltpu.make_async_copy(src, src, turn_s.at[j]).wait()

    grad_ref[...] = tile[...]


def owned_gradient(block_slot, activations, out_grad):
    dma = pltpu.SemaphoreType.DMA
    vmem = pl.BlockSpec(memory_space=pltpu.VMEM)
    return pl.pallas_call(
        gradient_kernel,
        name="owned_gradient",
        out_shape=jax.ShapeDtypeStruct((SIDE, SIDE), jnp.bfloat16),
        in_specs=[pl.BlockSpec(memory_space=pltpu.SMEM), vmem, vmem],
        out_specs=vmem,
        scratch_shapes=[
            pltpu.VMEM((NZ, 256, SIDE), jnp.bfloat16),
            pltpu.VMEM((4, 2, 8, FEAT, 256), jnp.bfloat16),
            pltpu.VMEM((256, 128), jnp.bfloat16),
            pltpu.VMEM((8 * FEAT, SIDE), jnp.float32),
            pltpu.VMEM((16, FEAT, 256), jnp.bfloat16),
            pltpu.VMEM((16, FEAT, 256), jnp.bfloat16),
            pltpu.VMEM((SIDE, SIDE), jnp.bfloat16),
            dma((2,)), dma((2,)), dma((2, 4, 2)), dma((2, 4, 2)), dma((4,)), dma((NZ,)), dma((16,)), dma((16,)),
            dma((8,)), dma((8,)), dma((16,)), dma((16,)), dma,
        ],
        compiler_params=pltpu.CompilerParams(collective_id=1, has_side_effects=True, vmem_limit_bytes=VMEM_LIMIT),
        cost_estimate=pl.CostEstimate(flops=2 * 512 * 512 * 2048, bytes_accessed=1 << 20, transcendentals=0),
    )(block_slot, activations, out_grad)


def matmul(left, right):
    return jnp.dot(left.astype(jnp.bfloat16), right.astype(jnp.bfloat16), preferred_element_type=jnp.float32)


def inverse_root(statistic):
    rows = lax.broadcasted_iota(jnp.int32, statistic.shape, 0)
    cols = lax.broadcasted_iota(jnp.int32, statistic.shape, 1)
    identity = jnp.where(rows == cols, 1.0, 0.0).astype(jnp.float32)
    scaling = 2.5 / jnp.sqrt(jnp.sum(statistic * statistic))

    def power(powered):
        dev = 0.25 * powered
        square = 1.5625 * identity - 2.5 * dev + matmul(dev, dev)
        return dev, matmul(matmul(square, square), powered)

    first, powered = power(statistic * scaling)
    second, powered = power(powered)
    third = 0.25 * powered
    pair = 1.25 * (first + second) - matmul(first, second)
    result = 1.953125 * identity - 1.25 * pair - 1.5625 * third + matmul(pair, third)
    return (result * jnp.sqrt(jnp.sqrt(scaling))).astype(jnp.bfloat16)


def slot_kernel(
    slots_ref, refresh_ref, grad_ref, lf_ref, rf_ref, lr_ref, rr_ref, dir_ref, nl_ref, nr_ref
):
    dp, mp = lax.axis_index("dp"), lax.axis_index("mp")
    mine = jnp.int32(0)
    for b in range(16):
        mine += jnp.where(slots_ref[mp, b] == dp, b, 0)
    hits = jnp.int32(0)
    for j in range(4):
        hits += jnp.where(refresh_ref[mp, j] == mine, 1, 0)

    @pl.when(hits > 0)
    def _():
        grad = grad_ref[...]
        left = lax.dot_general(grad, grad, (((1,), (1,)), ((), ())), preferred_element_type=jnp.float32)
        nl_ref[...] = inverse_root(0.9 * lf_ref[...] + left)
        right = lax.dot_general(grad, grad, (((0,), (0,)), ((), ())), preferred_element_type=jnp.float32)
        nr_ref[...] = inverse_root(0.9 * rf_ref[...] + right)

    @pl.when(hits == 0)
    def _():
        nl_ref[...] = lr_ref[...]
        nr_ref[...] = rr_ref[...]

    grad = grad_ref[...]
    mixed = jnp.dot(nl_ref[...], grad, preferred_element_type=jnp.float32).astype(jnp.bfloat16)
    precond = jnp.dot(mixed, nr_ref[...], preferred_element_type=jnp.float32)
    wide = grad.astype(jnp.float32)
    ratio = jnp.sqrt((jnp.sum(wide * wide) + 1e-06) / (jnp.sum(precond * precond) + 1e-06))
    dir_ref[...] = (precond * ratio).astype(jnp.bfloat16)


def slot_step(block_slot, refresh_list, gradient, left_factor, right_factor, left_root, right_root):
    vmem = pl.BlockSpec(memory_space=pltpu.VMEM)
    smem = pl.BlockSpec(memory_space=pltpu.SMEM)
    tile = jax.ShapeDtypeStruct((SIDE, SIDE), jnp.bfloat16)
    return pl.pallas_call(
        slot_kernel,
        name="slot_step",
        out_shape=(tile, tile, tile),
        in_specs=[smem, smem] + [vmem] * 5,
        out_specs=(vmem, vmem, vmem),
        compiler_params=pltpu.CompilerParams(vmem_limit_bytes=VMEM_LIMIT),
        cost_estimate=pl.CostEstimate(flops=2 * 512**3 * 20, bytes_accessed=5 << 20, transcendentals=0),
    )(block_slot, refresh_list, gradient, left_factor, right_factor, left_root, right_root)


def spread_kernel(
    tile_ref, every, z_s, z_r, zb_s, zb_r, y_s, y_r, yb_s, yb_r, local_s
):
    z, h, l, x, k = place()
    dp, mp = lax.axis_index("dp"), lax.axis_index("mp")
    ends = ((2 * ((z + 1) % NZ) + h, mp), (2 * ((z + NZ - 1) % NZ) + h, mp))
    partner = (2 * z + 1 - h, mp)
    barrier = pltpu.get_barrier_semaphore()
    for target in (*ends, partner):
        pl.semaphore_signal(barrier, inc=1, device_id=target, device_id_type=MESH)
    own = pltpu.make_async_copy(tile_ref, every.at[dp], local_s)
    own.start()
    pl.semaphore_wait(barrier, 3)

    pending = []

    def send(src, dst, ssem, rsem, target):
        copy = pltpu.make_async_remote_copy(
            src_ref=src, dst_ref=dst, send_sem=ssem, recv_sem=rsem, device_id=target, device_id_type=MESH
        )
        copy.start()
        pending.append(copy)

    def arrived(view, sem):
        pltpu.make_async_copy(view, view, sem).wait()

    def source(direction, step):
        return (z + NZ - step) % NZ if direction == 0 else (z + step) % NZ

    def a_rows(direction, step):
        if step < 3:
            return pl.ds(0, A_ROWS)
        return pl.ds(direction * HALF, HALF)

    def a_view(slot, rows):
        return every.at[slot, rows, :]

    def b_view(slot):
        return every.at[slot, pl.ds(A_ROWS, SIDE - A_ROWS), :]

    def z_a(direction, step):
        rows = a_rows(direction, step)
        dst = a_view(2 * source(direction, step) + h, rows)
        src = tile_ref.at[rows, :] if step == 0 else dst
        send(src, dst, z_s.at[direction, step], z_r.at[direction, step], ends[direction])

    def z_b(direction, step, u):
        dst = b_view(2 * source(direction, step) + u)
        src = dst
        send(src, dst, zb_s.at[direction, step, u], zb_r.at[direction, step, u], ends[direction])

    def y_a(index, slot, rows, src=None):
        dst = a_view(slot, rows)
        send(dst if src is None else src, dst, y_s.at[index], y_r.at[index], partner)

    full = pl.ds(0, A_ROWS)
    z_a(0, 0)
    z_a(1, 0)
    send(tile_ref.at[pl.ds(A_ROWS, SIDE - A_ROWS), :], b_view(dp), yb_s, yb_r, partner)
    y_a(0, dp, full, tile_ref.at[full, :])
    own.wait()
    z_b(0, 0, h)
    z_b(1, 0, h)
    arrived(b_view(2 * z + 1 - h), yb_r)
    z_b(0, 0, 1 - h)
    z_b(1, 0, 1 - h)

    for step in (1, 2, 3):
        for direction in (0, 1):
            slot = 2 * source(direction, step) + h
            arrived(a_view(slot, full), z_r.at[direction, step - 1])
            z_a(direction, step)
            y_a(1 + 3 * direction + step - 1, slot, full)
        for u in (h, 1 - h):
            for direction in (0, 1):
                arrived(b_view(2 * source(direction, step) + u), zb_r.at[direction, step - 1, u])
                if step < 3:
                    z_b(direction, step, u)
        if step == 3:
            z_b(0, 3, 0)
            z_b(1, 3, 1)
    for direction in (0, 1):
        rows = a_rows(direction, 3)
        slot = 2 * source(direction, 4) + h
        arrived(a_view(slot, rows), z_r.at[direction, 3])
        y_a(7 + direction, slot, rows)
    arrived(b_view(2 * source(0, 4)), zb_r.at[0, 3, 0])
    arrived(b_view(2 * source(1, 4) + 1), zb_r.at[1, 3, 1])

    other = 1 - h
    arrived(a_view(2 * z + other, full), y_r.at[0])
    for direction in (0, 1):
        for step in (1, 2, 3):
            arrived(a_view(2 * source(direction, step) + other, full), y_r.at[1 + 3 * direction + step - 1])
    for direction in (0, 1):
        arrived(a_view(2 * source(direction, 4) + other, a_rows(direction, 3)), y_r.at[7 + direction])
    for copy in pending:
        copy.wait_send()


def spread(tile):
    dma = pltpu.SemaphoreType.DMA
    return pl.pallas_call(
        spread_kernel,
        name="spread",
        out_shape=jax.ShapeDtypeStruct((16, SIDE, SIDE), jnp.bfloat16),
        in_specs=[pl.BlockSpec(memory_space=pl.ANY)],
        out_specs=pl.BlockSpec(memory_space=pl.ANY),
        scratch_shapes=[
            dma((2, 4)), dma((2, 4)), dma((2, 4, 2)), dma((2, 4, 2)), dma((9,)), dma((9,)), dma, dma, dma,
        ],
        compiler_params=pltpu.CompilerParams(collective_id=2, has_side_effects=True),
        cost_estimate=pl.CostEstimate(flops=0, bytes_accessed=16 << 20, transcendentals=0),
    )(tile)


def arrange_kernel(slots_ref, every, out_ref):
    out_ref[...] = every[0]


def arrange(slot_row, every):
    return pl.pallas_call(
        arrange_kernel,
        name="arrange",
        grid_spec=pltpu.PrefetchScalarGridSpec(
            num_scalar_prefetch=1,
            grid=(16,),
            in_specs=[pl.BlockSpec((1, SIDE, SIDE), lambda b, slots: (slots[b], 0, 0))],
            out_specs=pl.BlockSpec((SIDE, SIDE), lambda b, slots: (b // 2, b % 2)),
        ),
        out_shape=jax.ShapeDtypeStruct((8 * SIDE, 2 * SIDE), jnp.bfloat16),
        cost_estimate=pl.CostEstimate(flops=0, bytes_accessed=16 << 20, transcendentals=0),
    )(slot_row, every)


def body(
    activations,
    out_grad,
    block_slot,
    refresh_list,
    left_factor,
    right_factor,
    left_root,
    right_root,
):
    slot_row = lax.dynamic_index_in_dim(block_slot, lax.axis_index("mp"), 0, keepdims=False)
    gradient = owned_gradient(block_slot, activations, out_grad)
    tile, new_left, new_right = slot_step(
        block_slot, refresh_list, gradient,
        left_factor[0, 0], right_factor[0, 0], left_root[0, 0], right_root[0, 0],
    )
    direction = arrange(slot_row, spread(tile))
    return (direction, new_left[None, None], new_right[None, None])


def solution(mesh):
    in_specs = (
        P("dp", "mp"),
        P("dp", "mp"),
        P(),
        P(),
        P("dp", "mp", None, None),
        P("dp", "mp", None, None),
        P("dp", "mp", None, None),
        P("dp", "mp", None, None),
    )
    out_specs = (P(None, "mp"), P("dp", "mp", None, None), P("dp", "mp", None, None))
    return jax.shard_map(body, mesh=mesh, in_specs=in_specs, out_specs=out_specs, check_vma=False)
```

```python
import jax
import jax.numpy as jnp
from jax import lax
from jax.experimental import pallas as pl
from jax.experimental.pallas import tpu as pltpu
from jax.sharding import PartitionSpec as P

NZ, NX, NY = 8, 4, 4
SIDE = 512
FEAT = 64
A_ROWS = 288
HALF = A_ROWS // 2
MESH = pl.DeviceIdType.MESH
VMEM_LIMIT = 40 * 1024 * 1024


def place():
    dp, mp = lax.axis_index("dp"), lax.axis_index("mp")
    return dp // 2, dp % 2, mp // 8, (mp // 2) % 4, mp % 2


def device(z, h, l, x, k):
    return (2 * z + h, 8 * l + 2 * x + k)


def matmul(left, right):
    return jnp.dot(left.astype(jnp.bfloat16), right.astype(jnp.bfloat16), preferred_element_type=jnp.float32)


def inverse_roots(statistics):
    shape = statistics[0].shape
    rows = lax.broadcasted_iota(jnp.int32, shape, 0)
    cols = lax.broadcasted_iota(jnp.int32, shape, 1)
    identity = jnp.where(rows == cols, 1.0, 0.0).astype(jnp.float32)
    scaling = [2.5 / jnp.sqrt(jnp.sum(a * a)) for a in statistics]
    powered = [a * c for a, c in zip(statistics, scaling)]
    parts = []
    for _ in range(2):
        dev = [0.25 * m for m in powered]
        parts.append(dev)
        square = [1.5625 * identity - 2.5 * e + matmul(e, e) for e in dev]
        fourth = [matmul(f, f) for f in square]
        powered = [matmul(f, m) for f, m in zip(fourth, powered)]
    third = [0.25 * m for m in powered]
    pair = [1.25 * (e + f) - matmul(e, f) for e, f in zip(*parts)]
    result = [1.953125 * identity - 1.25 * p - 1.5625 * e + matmul(p, e) for p, e in zip(pair, third)]
    return [(x * jnp.sqrt(jnp.sqrt(c))).astype(jnp.bfloat16) for x, c in zip(result, scaling)]


def step_kernel(
    slots_hbm, refresh_hbm, act_hbm, out_hbm, lf_hbm, rf_hbm, lr_hbm, rr_hbm, every, nl_ref, nr_ref,
    slots_ref, refresh_ref, act_ref, out_ref, lf_ref, rf_ref, lr_ref, rr_ref, load_s, cot, act, flipped, total, pieces, outgoing, tile,
    swap_s, swap_r, ring_s, ring_r, turn_s, turn_r, plane_s, plane_r,
    pass_s, pass_r, give_s, give_r, local_s, z_s, z_r, zb_s, zb_r, y_s, y_r, yb_s, yb_r,
):
    z, h, l, x, k = place()
    dp, mp = lax.axis_index("dp"), lax.axis_index("mp")
    y = 2 * h + l
    r = 4 * l + x
    up, down = (z + 1) % NZ, (z + NZ - 1) % NZ

    loads = [
        pltpu.make_async_copy(src, dst, load_s.at[i])
        for i, (src, dst) in enumerate(
            (
                (act_hbm, act_ref), (out_hbm, out_ref), (slots_hbm, slots_ref), (refresh_hbm, refresh_ref),
                (lf_hbm, lf_ref), (rf_hbm, rf_ref), (lr_hbm, lr_ref), (rr_hbm, rr_ref),
            )
        )
    ]
    for copy in loads:
        copy.start()
    barrier = pltpu.get_barrier_semaphore()

    def greet(target):
        pl.semaphore_signal(barrier, inc=1, device_id=target, device_id_type=MESH)

    for step in range(1, 16):
        greet(((dp + step) % 16, mp))
    for dy in range(NY):
        for dx in range(NX):
            if (dy, dx) != (0, 0):
                ty, tx = (y + dy) % NY, (x + dx) % NX
                greet(device(z, ty // 2, ty % 2, tx, k))
    for step in range(NZ):
        greet(device((z + step) % NZ, h, l, x, 1 - k))

    for copy in loads[:4]:
        copy.wait()
    for c in range(2):
        cot[z, pl.ds(h * 128, 128), c * 256 : c * 256 + 256] = out_ref[
            :, pl.ds(pl.multiple_of(c * 512 + 256 * h, 256), 256)
        ]
    flipped[...] = act_ref[...].astype(jnp.float32).T.astype(jnp.bfloat16)
    pl.semaphore_wait(barrier, 38)

    def send(src, dst, ssem, rsem, target):
        copy = pltpu.make_async_remote_copy(
            src_ref=src, dst_ref=dst, send_sem=ssem, recv_sem=rsem, device_id=target, device_id_type=MESH
        )
        copy.start()
        return copy

    pending = []

    def turn_view(source):
        return act.at[source // 2, source % 2, r, :, pl.ds(pl.multiple_of(h * 128, 128), 128)]

    for j in range(4):
        target = 4 * k + j
        here = jnp.logical_and(target == z, z % 2 == k)
        src = flipped.at[j * FEAT : (j + 1) * FEAT, :]

        @pl.when(jnp.logical_not(here))
        def _():
            send(src, turn_view(z), turn_s.at[j], turn_r.at[z], device(target, h, l, x, z % 2))

        @pl.when(here)
        def _():
            pltpu.make_async_copy(src, turn_view(z), turn_r.at[z]).start()

    for c in range(2):
        pending.append(
            send(
                out_ref.at[:, pl.ds(pl.multiple_of(c * 512 + 256 * (1 - h), 256), 256)],
                cot.at[z, pl.ds(pl.multiple_of(h * 128, 128), 128), pl.ds(c * 256, 256)],
                swap_s.at[c], swap_r.at[c], (2 * z + 1 - h, mp),
            )
        )

    def unit(source, u):
        return cot.at[source, pl.ds(pl.multiple_of(u * 128, 128), 128), :]

    def ring(direction, step, u):
        source = (z + NZ - step) % NZ if direction == 0 else (z + step) % NZ
        target = up if direction == 0 else down
        view = unit(source, u)
        pending.append(
            send(view, view, ring_s.at[direction, step, u], ring_r.at[direction, step, u], (2 * target + h, mp))
        )

    def ring_wait(direction, step, u):
        source = (z + NZ - step) % NZ if direction == 0 else (z + step) % NZ
        view = unit(source, u)
        pltpu.make_async_remote_copy(
            src_ref=view, dst_ref=view, send_sem=ring_s.at[direction, step - 1, u],
            recv_sem=ring_r.at[direction, step - 1, u], device_id=(dp, mp), device_id_type=MESH,
        ).wait_recv()

    ring(0, 0, h)
    ring(1, 0, h)

    for i in range(4):
        source = 2 * i + k
        view = turn_view(source)
        pltpu.make_async_copy(view, view, turn_r.at[source]).wait()

    def plane_view(row, half):
        return act.at[:, k, row, :, pl.ds(pl.multiple_of(half * 128, 128), 128)]

    for dy in range(NY):
        for dx in range(NX):
            if (dy, dx) != (0, 0):
                ty, tx = (y + dy) % NY, (x + dx) % NX
                view = plane_view(r, h)
                pending.append(
                    send(view, view, plane_s.at[4 * dy + dx], plane_r.at[4 * dy + dx], device(z, ty // 2, ty % 2, tx, k))
                )

    for c in range(2):
        view = cot.at[z, pl.ds(pl.multiple_of((1 - h) * 128, 128), 128), pl.ds(c * 256, 256)]
        pltpu.make_async_copy(view, view, swap_r.at[c]).wait()
    ring(0, 0, 1 - h)
    ring(1, 0, 1 - h)

    for step in (1, 2):
        for u in (h, 1 - h):
            for direction in (0, 1):
                ring_wait(direction, step, u)
                ring(direction, step, u)

    for dy in range(NY):
        for dx in range(NX):
            if (dy, dx) != (0, 0):
                sy, sx = (y + NY - dy) % NY, (x + NX - dx) % NX
                view = plane_view(4 * (sy % 2) + sx, sy // 2)
                pltpu.make_async_copy(view, view, plane_r.at[4 * dy + dx]).wait()
    for row in range(8):
        view = act.at[:, k, row]
        pending.append(send(view, view, pass_s.at[row], pass_r.at[row], device(z, h, l, x, 1 - k)))

    for u in (h, 1 - h):
        for direction in (0, 1):
            ring_wait(direction, 3, u)
    ring(0, 3, 0)
    ring(1, 3, 1)

    for row in range(8):
        view = act.at[:, 1 - k, row]
        pltpu.make_async_copy(view, view, pass_r.at[row]).wait()

    def product(source):
        return jnp.dot(
            act[source // 2, source % 2].reshape(8 * FEAT, 256), cot[source], preferred_element_type=jnp.float32
        )

    total[...] = product(z)

    @pl.loop(1, 4)
    def _(step):
        total[...] += product((z + step) % NZ)
        total[...] += product((z + NZ - step) % NZ)

    ring_wait(0, 4, 0)
    ring_wait(1, 4, 1)
    total[...] += product((z + 4) % NZ)

    for row in range(8):
        for c in range(2):
            pieces[2 * row + c] = total[row * FEAT : (row + 1) * FEAT, c * 256 : (c + 1) * 256].astype(jnp.bfloat16)

    def spot(slot):
        return tile.at[
            pl.ds(pl.multiple_of((slot // 2) * FEAT, FEAT), FEAT), pl.ds(pl.multiple_of((slot % 2) * 256, 256), 256)
        ]

    def held(slot):
        found = jnp.int32(0)
        for b in range(16):
            found = jnp.maximum(found, jnp.where(slots_ref[mp, b] == slot, b, 0))
        return found

    @pl.loop(1, 16)
    def _(step):
        slot = (dp + step) % 16
        outgoing[slot] = pieces[held(slot)]
        send(outgoing.at[slot], spot(dp), give_s.at[slot], give_r.at[dp], (slot, mp))

    outgoing[dp] = pieces[held(dp)]
    own = pltpu.make_async_copy(outgoing.at[dp], spot(dp), local_s)
    own.start()
    own.wait()

    @pl.loop(1, 16)
    def _(step):
        slot = (dp + step) % 16
        view = spot(slot)
        pltpu.make_async_copy(view, view, give_r.at[slot]).wait()
        pltpu.make_async_copy(outgoing.at[slot], outgoing.at[slot], give_s.at[slot]).wait()

    for copy in loads[4:]:
        copy.wait()
    mine = held(dp)
    hits = jnp.int32(0)
    for j in range(4):
        hits += jnp.where(refresh_ref[j, mp] == mine, 1, 0)
    chosen = jnp.broadcast_to(hits > 0, (SIDE, SIDE))
    grad = tile[...]
    left = lax.dot_general(grad, grad, (((1,), (1,)), ((), ())), preferred_element_type=jnp.float32)
    right = lax.dot_general(grad, grad, (((0,), (0,)), ((), ())), preferred_element_type=jnp.float32)
    lroot, rroot = inverse_roots((0.9 * lf_ref[...] + left, 0.9 * rf_ref[...] + right))
    nl_ref[...] = jnp.where(chosen, lroot, lr_ref[...])
    nr_ref[...] = jnp.where(chosen, rroot, rr_ref[...])
    mixed = jnp.dot(nl_ref[...], grad, preferred_element_type=jnp.float32).astype(jnp.bfloat16)
    precond = jnp.dot(mixed, nr_ref[...], preferred_element_type=jnp.float32)
    wide = grad.astype(jnp.float32)
    ratio = jnp.sqrt((jnp.sum(wide * wide) + 1e-06) / (jnp.sum(precond * precond) + 1e-06))
    every[dp] = (precond * ratio).astype(jnp.bfloat16)

    ends = ((2 * up + h, mp), (2 * down + h, mp))
    partner = (2 * z + 1 - h, mp)

    def arrived(view, sem):
        pltpu.make_async_copy(view, view, sem).wait()

    def source(direction, step):
        return (z + NZ - step) % NZ if direction == 0 else (z + step) % NZ

    def a_rows(direction, step):
        if step < 3:
            return pl.ds(0, A_ROWS)
        return pl.ds(direction * HALF, HALF)

    def post(src, dst, ssem, rsem, target):
        pending.append(send(src, dst, ssem, rsem, target))

    def a_view(slot, rows):
        return every.at[slot, rows, :]

    def b_view(slot):
        return every.at[slot, pl.ds(A_ROWS, SIDE - A_ROWS), :]

    def z_a(direction, step):
        rows = a_rows(direction, step)
        dst = a_view(2 * source(direction, step) + h, rows)
        src = dst
        post(src, dst, z_s.at[direction, step], z_r.at[direction, step], ends[direction])

    def z_b(direction, step, u):
        dst = b_view(2 * source(direction, step) + u)
        src = dst
        post(src, dst, zb_s.at[direction, step, u], zb_r.at[direction, step, u], ends[direction])

    def y_a(index, slot, rows):
        dst = a_view(slot, rows)
        post(dst, dst, y_s.at[index], y_r.at[index], partner)

    full = pl.ds(0, A_ROWS)
    z_a(0, 0)
    z_a(1, 0)
    post(b_view(dp), b_view(dp), yb_s, yb_r, partner)
    y_a(0, dp, full)
    z_b(0, 0, h)
    z_b(1, 0, h)
    arrived(b_view(2 * z + 1 - h), yb_r)
    z_b(0, 0, 1 - h)
    z_b(1, 0, 1 - h)

    for step in (1, 2, 3):
        for direction in (0, 1):
            slot = 2 * source(direction, step) + h
            arrived(a_view(slot, full), z_r.at[direction, step - 1])
            z_a(direction, step)
            y_a(1 + 3 * direction + step - 1, slot, full)
        for u in (h, 1 - h):
            for direction in (0, 1):
                arrived(b_view(2 * source(direction, step) + u), zb_r.at[direction, step - 1, u])
                if step < 3:
                    z_b(direction, step, u)
        if step == 3:
            z_b(0, 3, 0)
            z_b(1, 3, 1)
    for direction in (0, 1):
        rows = a_rows(direction, 3)
        slot = 2 * source(direction, 4) + h
        arrived(a_view(slot, rows), z_r.at[direction, 3])
        y_a(7 + direction, slot, rows)
    arrived(b_view(2 * source(0, 4)), zb_r.at[0, 3, 0])
    arrived(b_view(2 * source(1, 4) + 1), zb_r.at[1, 3, 1])

    other = 1 - h
    arrived(a_view(2 * z + other, full), y_r.at[0])
    for direction in (0, 1):
        for step in (1, 2, 3):
            arrived(a_view(2 * source(direction, step) + other, full), y_r.at[1 + 3 * direction + step - 1])
    for direction in (0, 1):
        arrived(a_view(2 * source(direction, 4) + other, a_rows(direction, 3)), y_r.at[7 + direction])

    for copy in pending:
        copy.wait_send()
    for j in range(4):
        here = jnp.logical_and(4 * k + j == z, z % 2 == k)
        src = flipped.at[j * FEAT : (j + 1) * FEAT, :]

        @pl.when(jnp.logical_not(here))
        def _():
            pltpu.make_async_copy(src, src, turn_s.at[j]).wait()


def step(block_slot, refresh_list, activations, out_grad, left_factor, right_factor, left_root, right_root):
    dma = pltpu.SemaphoreType.DMA
    vmem = pl.BlockSpec(memory_space=pltpu.VMEM)
    tile = jax.ShapeDtypeStruct((SIDE, SIDE), jnp.bfloat16)
    return pl.pallas_call(
        step_kernel,
        name="step",
        out_shape=(jax.ShapeDtypeStruct((16, SIDE, SIDE), jnp.bfloat16), tile, tile),
        in_specs=[pl.BlockSpec(memory_space=pltpu.HBM)] * 8,
        out_specs=(vmem, vmem, vmem),
        scratch_shapes=[
            pltpu.SMEM((16, 16), jnp.int32),
            pltpu.SMEM((4, 16), jnp.int32),
            pltpu.VMEM((128, 256), jnp.bfloat16),
            pltpu.VMEM((128, 1024), jnp.bfloat16),
            pltpu.VMEM((SIDE, SIDE), jnp.float32),
            pltpu.VMEM((SIDE, SIDE), jnp.float32),
            pltpu.VMEM((SIDE, SIDE), jnp.bfloat16),
            pltpu.VMEM((SIDE, SIDE), jnp.bfloat16),
            dma((8,)),
            pltpu.VMEM((NZ, 256, SIDE), jnp.bfloat16),
            pltpu.VMEM((4, 2, 8, FEAT, 256), jnp.bfloat16),
            pltpu.VMEM((256, 128), jnp.bfloat16),
            pltpu.VMEM((8 * FEAT, SIDE), jnp.float32),
            pltpu.VMEM((16, FEAT, 256), jnp.bfloat16),
            pltpu.VMEM((16, FEAT, 256), jnp.bfloat16),
            pltpu.VMEM((SIDE, SIDE), jnp.bfloat16),
            dma((2,)), dma((2,)), dma((2, 4, 2)), dma((2, 4, 2)), dma((4,)), dma((NZ,)), dma((16,)), dma((16,)),
            dma((8,)), dma((8,)), dma((16,)), dma((16,)), dma,
            dma((2, 4)), dma((2, 4)), dma((2, 4, 2)), dma((2, 4, 2)), dma((9,)), dma((9,)), dma, dma,
        ],
        compiler_params=pltpu.CompilerParams(collective_id=1, has_side_effects=True, vmem_limit_bytes=VMEM_LIMIT),
        cost_estimate=pl.CostEstimate(flops=2 * 512**3 * 24, bytes_accessed=20 << 20, transcendentals=0),
    )(*(
        pltpu.with_memory_space_constraint(x, pltpu.HBM)
        for x in (block_slot, refresh_list.T, activations, out_grad, left_factor, right_factor, left_root, right_root)
    ))


def arrange_kernel(slots_hbm, every, left, right, out_hbm, nl_hbm, nr_hbm, slots_ref, sem):
    mp = lax.axis_index("mp")
    load = pltpu.make_async_copy(slots_hbm, slots_ref, sem.at[16])
    load.start()
    copies = [
        pltpu.make_async_copy(left, nl_hbm, sem.at[17]),
        pltpu.make_async_copy(right, nr_hbm, sem.at[18]),
    ]
    for copy in copies:
        copy.start()
    load.wait()
    for b in range(16):
        copy = pltpu.make_async_copy(
            every.at[slots_ref[mp, b]],
            out_hbm.at[pl.ds((b // 2) * SIDE, SIDE), pl.ds((b % 2) * SIDE, SIDE)],
            sem.at[b],
        )
        copy.start()
        copies.append(copy)
    for copy in copies:
        copy.wait()


def arrange(block_slot, every, left, right):
    hbm = pl.BlockSpec(memory_space=pltpu.HBM)
    vmem = pl.BlockSpec(memory_space=pltpu.VMEM)
    tile = jax.ShapeDtypeStruct((SIDE, SIDE), jnp.bfloat16)
    return pl.pallas_call(
        arrange_kernel,
        name="arrange",
        in_specs=[hbm, vmem, vmem, vmem],
        out_specs=(hbm, hbm, hbm),
        out_shape=(jax.ShapeDtypeStruct((8 * SIDE, 2 * SIDE), jnp.bfloat16), tile, tile),
        scratch_shapes=[pltpu.SMEM((16, 16), jnp.int32), pltpu.SemaphoreType.DMA((19,))],
        compiler_params=pltpu.CompilerParams(vmem_limit_bytes=VMEM_LIMIT),
        cost_estimate=pl.CostEstimate(flops=0, bytes_accessed=16 << 20, transcendentals=0),
    )(pltpu.with_memory_space_constraint(block_slot, pltpu.HBM), every, left, right)


def body(
    activations,
    out_grad,
    block_slot,
    refresh_list,
    left_factor,
    right_factor,
    left_root,
    right_root,
):
    every, new_left, new_right = step(
        block_slot, refresh_list, activations, out_grad,
        left_factor[0, 0], right_factor[0, 0], left_root[0, 0], right_root[0, 0],
    )
    direction, new_left, new_right = arrange(block_slot, every, new_left, new_right)
    return (direction, new_left[None, None], new_right[None, None])


def solution(mesh):
    in_specs = (
        P("dp", "mp"),
        P("dp", "mp"),
        P(),
        P(),
        P("dp", "mp", None, None),
        P("dp", "mp", None, None),
        P("dp", "mp", None, None),
        P("dp", "mp", None, None),
    )
    out_specs = (P(None, "mp"), P("dp", "mp", None, None), P("dp", "mp", None, None))
    return jax.shard_map(body, mesh=mesh, in_specs=in_specs, out_specs=out_specs, check_vma=False)
```

```python
import jax
import jax.numpy as jnp
from jax import lax
from jax.experimental import pallas as pl
from jax.experimental.pallas import tpu as pltpu
from jax.sharding import PartitionSpec as P

NZ, NX, NY = 8, 4, 4
SIDE = 512
FEAT = 64
A_ROWS = 288
HALF = A_ROWS // 2
MESH = pl.DeviceIdType.MESH
VMEM_LIMIT = 40 * 1024 * 1024


def place():
    dp, mp = lax.axis_index("dp"), lax.axis_index("mp")
    return dp // 2, dp % 2, mp // 8, (mp // 2) % 4, mp % 2


def device(z, h, l, x, k):
    return (2 * z + h, 8 * l + 2 * x + k)


def matmul(left, right):
    return jnp.dot(left.astype(jnp.bfloat16), right.astype(jnp.bfloat16), preferred_element_type=jnp.float32)


def inverse_roots(statistics):
    shape = statistics[0].shape
    rows = lax.broadcasted_iota(jnp.int32, shape, 0)
    cols = lax.broadcasted_iota(jnp.int32, shape, 1)
    identity = jnp.where(rows == cols, 1.0, 0.0).astype(jnp.float32)
    scaling = [2.5 / jnp.sqrt(jnp.sum(a * a)) for a in statistics]
    powered = [a * c for a, c in zip(statistics, scaling)]
    parts = []
    for _ in range(2):
        dev = [0.25 * m for m in powered]
        parts.append(dev)
        square = [1.5625 * identity - 2.5 * e + matmul(e, e) for e in dev]
        fourth = [matmul(f, f) for f in square]
        powered = [matmul(f, m) for f, m in zip(fourth, powered)]
    third = [0.25 * m for m in powered]
    pair = [1.25 * (e + f) - matmul(e, f) for e, f in zip(*parts)]
    result = [1.953125 * identity - 1.25 * p - 1.5625 * e + matmul(p, e) for p, e in zip(pair, third)]
    return [(x * jnp.sqrt(jnp.sqrt(c))).astype(jnp.bfloat16) for x, c in zip(result, scaling)]


def step_kernel(
    slots_hbm, refresh_hbm, act_hbm, out_hbm, lf_hbm, rf_hbm, lr_hbm, rr_hbm, every, nl_ref, nr_ref,
    slots_ref, refresh_ref, act_ref, out_ref, lf_ref, rf_ref, lr_ref, rr_ref, load_s, cot, act, flipped, total, table, outgoing, tile,
    swap_s, swap_r, ring_s, ring_r, turn_s, turn_r, plane_s, plane_r,
    pass_s, pass_r, give_s, give_r, local_s, z_s, z_r, zb_s, zb_r, y_s, y_r, yb_s, yb_r,
):
    z, h, l, x, k = place()
    dp, mp = lax.axis_index("dp"), lax.axis_index("mp")
    y = 2 * h + l
    up, down = (z + 1) % NZ, (z + NZ - 1) % NZ

    loads = [
        pltpu.make_async_copy(src, dst, load_s.at[i])
        for i, (src, dst) in enumerate(
            (
                (act_hbm, act_ref), (out_hbm, out_ref), (slots_hbm, slots_ref), (refresh_hbm, refresh_ref),
                (lf_hbm, lf_ref), (rf_hbm, rf_ref), (lr_hbm, lr_ref), (rr_hbm, rr_ref),
            )
        )
    ]
    for copy in loads:
        copy.start()
    barrier = pltpu.get_barrier_semaphore()

    def x_peer(step):
        return device(z, h, l, (x + step) % NX, k)

    def y_peer(step):
        there = (y + step) % NY
        return device(z, there // 2, there % 2, x, k)

    def greet(target):
        pl.semaphore_signal(barrier, inc=1, device_id=target, device_id_type=MESH)

    for step in range(1, NZ):
        greet(device((z + step) % NZ, h, l, x, k))
    for step in range(NZ):
        greet(device((z + step) % NZ, h, l, x, 1 - k))
    for step in range(1, 4):
        greet(x_peer(step))
        greet(y_peer(step))

    for copy in loads[:4]:
        copy.wait()
    for c in range(2):
        cot[z, pl.ds(h * 128, 128), c * 256 : c * 256 + 256] = out_ref[
            :, pl.ds(pl.multiple_of(c * 512 + 256 * h, 256), 256)
        ]
    pl.semaphore_wait(barrier, 21)

    def send(src, dst, ssem, rsem, target):
        copy = pltpu.make_async_remote_copy(
            src_ref=src, dst_ref=dst, send_sem=ssem, recv_sem=rsem, device_id=target, device_id_type=MESH
        )
        copy.start()
        return copy

    pending = []

    for c in range(2):
        pending.append(
            send(
                out_ref.at[:, pl.ds(pl.multiple_of(c * 512 + 256 * (1 - h), 256), 256)],
                cot.at[z, pl.ds(pl.multiple_of(h * 128, 128), 128), pl.ds(c * 256, 256)],
                swap_s.at[c], swap_r.at[c], (2 * z + 1 - h, mp),
            )
        )

    def unit(source, u):
        return cot.at[source, pl.ds(pl.multiple_of(u * 128, 128), 128), :]

    def ring(direction, step, u):
        source = (z + NZ - step) % NZ if direction == 0 else (z + step) % NZ
        target = up if direction == 0 else down
        view = unit(source, u)
        pending.append(
            send(view, view, ring_s.at[direction, step, u], ring_r.at[direction, step, u], (2 * target + h, mp))
        )

    def ring_wait(direction, step, u):
        source = (z + NZ - step) % NZ if direction == 0 else (z + step) % NZ
        view = unit(source, u)
        pltpu.make_async_remote_copy(
            src_ref=view, dst_ref=view, send_sem=ring_s.at[direction, step - 1, u],
            recv_sem=ring_r.at[direction, step - 1, u], device_id=(dp, mp), device_id_type=MESH,
        ).wait_recv()

    ring(0, 0, h)
    ring(1, 0, h)


    flipped[...] = act_ref[...].astype(jnp.float32).T.astype(jnp.bfloat16)

    def turn_view(source):
        return act.at[source // 2, source % 2, l, x, :, pl.ds(pl.multiple_of(h * 128, 128), 128)]

    for j in range(4):
        target = 4 * k + j
        here = jnp.logical_and(target == z, z % 2 == k)
        src = flipped.at[j * FEAT : (j + 1) * FEAT, :]

        @pl.when(jnp.logical_not(here))
        def _():
            send(src, turn_view(z), turn_s.at[j], turn_r.at[z], device(target, h, l, x, z % 2))

        @pl.when(here)
        def _():
            pltpu.make_async_copy(src, turn_view(z), turn_r.at[z]).start()

    for c in range(2):
        view = cot.at[z, pl.ds(pl.multiple_of((1 - h) * 128, 128), 128), pl.ds(c * 256, 256)]
        pltpu.make_async_copy(view, view, swap_r.at[c]).wait()
    ring(0, 0, 1 - h)
    ring(1, 0, 1 - h)

    for i in range(4):
        source = 2 * i + k
        view = turn_view(source)
        pltpu.make_async_copy(view, view, turn_r.at[source]).wait()

    def tokens(half):
        return pl.ds(pl.multiple_of(half * 128, 128), 128)

    def first_view(part, col, row):
        return act.at[2 * part : 2 * part + 2, k, row % 2, col, :, tokens(row // 2)]

    def second_view(part, index):
        if part == 0:
            return act.at[0:2, k, index % 2, :, :, tokens(index // 2)]
        return act.at[2:4, k, :, index]

    def peer(axis, step):
        return x_peer(step) if axis == 0 else y_peer(step)

    def back(axis, step):
        return (x + NX - step) % NX if axis == 0 else (y + NY - step) % NY

    for step in (1, 2, 3):
        for part in (0, 1):
            view = first_view(part, x, y)
            pending.append(send(view, view, plane_s.at[0, part, step], plane_r.at[0, part, step], peer(part, step)))

    def advance(step):
        for u in (h, 1 - h):
            for direction in (0, 1):
                ring_wait(direction, step, u)
                ring(direction, step, u)

    advance(1)
    for part in (0, 1):
        for step in (1, 2, 3):
            view = first_view(0, back(0, step), y) if part == 0 else first_view(1, x, back(1, step))
            pltpu.make_async_copy(view, view, plane_r.at[0, part, step]).wait()
        view = second_view(part, y if part == 0 else x)
        for step in (1, 2, 3):
            pending.append(
                send(view, view, plane_s.at[1, part, step], plane_r.at[1, part, step], peer(1 - part, step))
            )
    advance(2)

    for part in (0, 1):
        for step in (1, 2, 3):
            view = second_view(part, back(1 - part, step))
            pltpu.make_async_copy(view, view, plane_r.at[1, part, step]).wait()
        view = act.at[2 * part : 2 * part + 2, k]
        pending.append(send(view, view, pass_s.at[part], pass_r.at[part], device(z, h, l, x, 1 - k)))

    def held(slot):
        found = jnp.int32(0)
        for b in range(16):
            found = jnp.maximum(found, jnp.where(slots_ref[mp, b] == slot, b, 0))
        return found

    for slot in range(16):
        table[slot] = held(slot)

    for u in (h, 1 - h):
        for direction in (0, 1):
            ring_wait(direction, 3, u)
    ring(0, 3, 0)
    ring(1, 3, 1)

    for part in (0, 1):
        view = act.at[2 * part : 2 * part + 2, 1 - k]
        pltpu.make_async_copy(view, view, pass_r.at[part]).wait()

    def product(source):
        return jnp.dot(
            act[source // 2, source % 2].reshape(8 * FEAT, 256), cot[source], preferred_element_type=jnp.float32
        )

    def add(value):
        for c in range(2):
            total[:, c] += value[:, c * 256 : (c + 1) * 256].reshape(8, FEAT, 256)

    total[...] = jnp.zeros_like(total)
    add(product(z))

    @pl.loop(1, 4)
    def _(step):
        add(product((z + step) % NZ) + product((z + NZ - step) % NZ))

    ring_wait(0, 4, 0)
    ring_wait(1, 4, 1)
    add(product((z + 4) % NZ))

    def piece(slot):
        block = table[slot]
        return total[block // 2, block % 2].astype(jnp.bfloat16)

    def spot(slot):
        return tile.at[
            pl.ds(pl.multiple_of((slot // 2) * FEAT, FEAT), FEAT), pl.ds(pl.multiple_of((slot % 2) * 256, 256), 256)
        ]

    @pl.loop(1, 16)
    def _(step):
        slot = (dp + step) % 16
        outgoing[slot] = piece(slot)
        send(outgoing.at[slot], spot(dp), give_s.at[slot], give_r.at[dp], (slot, mp))

    outgoing[dp] = piece(dp)
    own = pltpu.make_async_copy(outgoing.at[dp], spot(dp), local_s)
    own.start()
    own.wait()

    @pl.loop(1, 16)
    def _(step):
        slot = (dp + step) % 16
        view = spot(slot)
        pltpu.make_async_copy(view, view, give_r.at[slot]).wait()

    for copy in loads[4:]:
        copy.wait()
    mine = table[dp]
    hits = jnp.int32(0)
    for j in range(4):
        hits += jnp.where(refresh_ref[j, mp] == mine, 1, 0)
    chosen = jnp.broadcast_to(hits > 0, (SIDE, SIDE))
    grad = tile[...]
    left = lax.dot_general(grad, grad, (((1,), (1,)), ((), ())), preferred_element_type=jnp.float32)
    right = lax.dot_general(grad, grad, (((0,), (0,)), ((), ())), preferred_element_type=jnp.float32)
    lroot, rroot = inverse_roots((0.9 * lf_ref[...] + left, 0.9 * rf_ref[...] + right))
    nl_ref[...] = jnp.where(chosen, lroot, lr_ref[...])
    nr_ref[...] = jnp.where(chosen, rroot, rr_ref[...])
    mixed = jnp.dot(nl_ref[...], grad, preferred_element_type=jnp.float32).astype(jnp.bfloat16)
    precond = jnp.dot(mixed, nr_ref[...], preferred_element_type=jnp.float32)
    wide = grad.astype(jnp.float32)
    ratio = jnp.sqrt((jnp.sum(wide * wide) + 1e-06) / (jnp.sum(precond * precond) + 1e-06))
    every[dp] = (precond * ratio).astype(jnp.bfloat16)

    ends = ((2 * up + h, mp), (2 * down + h, mp))
    partner = (2 * z + 1 - h, mp)

    def arrived(view, sem):
        pltpu.make_async_copy(view, view, sem).wait()

    def source(direction, step):
        return (z + NZ - step) % NZ if direction == 0 else (z + step) % NZ

    def a_rows(direction, step):
        if step < 3:
            return pl.ds(0, A_ROWS)
        return pl.ds(direction * HALF, HALF)

    def post(src, dst, ssem, rsem, target):
        pending.append(send(src, dst, ssem, rsem, target))

    def a_view(slot, rows):
        return every.at[slot, rows, :]

    def b_view(slot):
        return every.at[slot, pl.ds(A_ROWS, SIDE - A_ROWS), :]

    def z_a(direction, step):
        rows = a_rows(direction, step)
        dst = a_view(2 * source(direction, step) + h, rows)
        src = dst
        post(src, dst, z_s.at[direction, step], z_r.at[direction, step], ends[direction])

    def z_b(direction, step, u):
        dst = b_view(2 * source(direction, step) + u)
        src = dst
        post(src, dst, zb_s.at[direction, step, u], zb_r.at[direction, step, u], ends[direction])

    def y_a(index, slot, rows):
        dst = a_view(slot, rows)
        post(dst, dst, y_s.at[index], y_r.at[index], partner)

    full = pl.ds(0, A_ROWS)
    z_a(0, 0)
    z_a(1, 0)
    post(b_view(dp), b_view(dp), yb_s, yb_r, partner)
    y_a(0, dp, full)
    z_b(0, 0, h)
    z_b(1, 0, h)
    arrived(b_view(2 * z + 1 - h), yb_r)
    z_b(0, 0, 1 - h)
    z_b(1, 0, 1 - h)

    for step in (1, 2, 3):
        for direction in (0, 1):
            slot = 2 * source(direction, step) + h
            arrived(a_view(slot, full), z_r.at[direction, step - 1])
            z_a(direction, step)
            y_a(1 + 3 * direction + step - 1, slot, full)
        for u in (h, 1 - h):
            for direction in (0, 1):
                arrived(b_view(2 * source(direction, step) + u), zb_r.at[direction, step - 1, u])
                if step < 3:
                    z_b(direction, step, u)
        if step == 3:
            z_b(0, 3, 0)
            z_b(1, 3, 1)
    for direction in (0, 1):
        rows = a_rows(direction, 3)
        slot = 2 * source(direction, 4) + h
        arrived(a_view(slot, rows), z_r.at[direction, 3])
        y_a(7 + direction, slot, rows)
    arrived(b_view(2 * source(0, 4)), zb_r.at[0, 3, 0])
    arrived(b_view(2 * source(1, 4) + 1), zb_r.at[1, 3, 1])

    other = 1 - h
    arrived(a_view(2 * z + other, full), y_r.at[0])
    for direction in (0, 1):
        for step in (1, 2, 3):
            arrived(a_view(2 * source(direction, step) + other, full), y_r.at[1 + 3 * direction + step - 1])
    for direction in (0, 1):
        arrived(a_view(2 * source(direction, 4) + other, a_rows(direction, 3)), y_r.at[7 + direction])

    for copy in pending:
        copy.wait_send()

    @pl.loop(1, 16)
    def _(step):
        slot = (dp + step) % 16
        pltpu.make_async_copy(outgoing.at[slot], outgoing.at[slot], give_s.at[slot]).wait()

    for j in range(4):
        here = jnp.logical_and(4 * k + j == z, z % 2 == k)
        src = flipped.at[j * FEAT : (j + 1) * FEAT, :]

        @pl.when(jnp.logical_not(here))
        def _():
            pltpu.make_async_copy(src, src, turn_s.at[j]).wait()


def step(block_slot, refresh_list, activations, out_grad, left_factor, right_factor, left_root, right_root):
    dma = pltpu.SemaphoreType.DMA
    vmem = pl.BlockSpec(memory_space=pltpu.VMEM)
    tile = jax.ShapeDtypeStruct((SIDE, SIDE), jnp.bfloat16)
    return pl.pallas_call(
        step_kernel,
        name="step",
        out_shape=(jax.ShapeDtypeStruct((16, SIDE, SIDE), jnp.bfloat16), tile, tile),
        in_specs=[pl.BlockSpec(memory_space=pltpu.HBM)] * 8,
        out_specs=(vmem, vmem, vmem),
        scratch_shapes=[
            pltpu.SMEM((16, 16), jnp.int32),
            pltpu.SMEM((4, 16), jnp.int32),
            pltpu.VMEM((128, 256), jnp.bfloat16),
            pltpu.VMEM((128, 1024), jnp.bfloat16),
            pltpu.VMEM((SIDE, SIDE), jnp.float32),
            pltpu.VMEM((SIDE, SIDE), jnp.float32),
            pltpu.VMEM((SIDE, SIDE), jnp.bfloat16),
            pltpu.VMEM((SIDE, SIDE), jnp.bfloat16),
            dma((8,)),
            pltpu.VMEM((NZ, 256, SIDE), jnp.bfloat16),
            pltpu.VMEM((4, 2, 2, NX, FEAT, 256), jnp.bfloat16),
            pltpu.VMEM((256, 128), jnp.bfloat16),
            pltpu.VMEM((8, 2, FEAT, 256), jnp.float32),
            pltpu.SMEM((16,), jnp.int32),
            pltpu.VMEM((16, FEAT, 256), jnp.bfloat16),
            pltpu.VMEM((SIDE, SIDE), jnp.bfloat16),
            dma((2,)), dma((2,)), dma((2, 4, 2)), dma((2, 4, 2)), dma((4,)), dma((NZ,)), dma((2, 2, 4)), dma((2, 2, 4)),
            dma((2,)), dma((2,)), dma((16,)), dma((16,)), dma,
            dma((2, 4)), dma((2, 4)), dma((2, 4, 2)), dma((2, 4, 2)), dma((9,)), dma((9,)), dma, dma,
        ],
        compiler_params=pltpu.CompilerParams(collective_id=1, has_side_effects=True, vmem_limit_bytes=VMEM_LIMIT),
        cost_estimate=pl.CostEstimate(flops=2 * 512**3 * 24, bytes_accessed=20 << 20, transcendentals=0),
    )(*(
        pltpu.with_memory_space_constraint(x, pltpu.HBM)
        for x in (block_slot, refresh_list.T, activations, out_grad, left_factor, right_factor, left_root, right_root)
    ))


def arrange_kernel(slots_hbm, every, left, right, out_hbm, nl_hbm, nr_hbm, slots_ref, sem):
    mp = lax.axis_index("mp")
    load = pltpu.make_async_copy(slots_hbm, slots_ref, sem.at[16])
    load.start()
    copies = [
        pltpu.make_async_copy(left, nl_hbm, sem.at[17]),
        pltpu.make_async_copy(right, nr_hbm, sem.at[18]),
    ]
    for copy in copies:
        copy.start()
    load.wait()
    for b in range(16):
        copy = pltpu.make_async_copy(
            every.at[slots_ref[mp, b]],
            out_hbm.at[pl.ds((b // 2) * SIDE, SIDE), pl.ds((b % 2) * SIDE, SIDE)],
            sem.at[b],
        )
        copy.start()
        copies.append(copy)
    for copy in copies:
        copy.wait()


def arrange(block_slot, every, left, right):
    hbm = pl.BlockSpec(memory_space=pltpu.HBM)
    vmem = pl.BlockSpec(memory_space=pltpu.VMEM)
    tile = jax.ShapeDtypeStruct((SIDE, SIDE), jnp.bfloat16)
    return pl.pallas_call(
        arrange_kernel,
        name="arrange",
        in_specs=[hbm, vmem, vmem, vmem],
        out_specs=(hbm, hbm, hbm),
        out_shape=(jax.ShapeDtypeStruct((8 * SIDE, 2 * SIDE), jnp.bfloat16), tile, tile),
        scratch_shapes=[pltpu.SMEM((16, 16), jnp.int32), pltpu.SemaphoreType.DMA((19,))],
        compiler_params=pltpu.CompilerParams(vmem_limit_bytes=VMEM_LIMIT),
        cost_estimate=pl.CostEstimate(flops=0, bytes_accessed=16 << 20, transcendentals=0),
    )(pltpu.with_memory_space_constraint(block_slot, pltpu.HBM), every, left, right)


def body(
    activations,
    out_grad,
    block_slot,
    refresh_list,
    left_factor,
    right_factor,
    left_root,
    right_root,
):
    every, new_left, new_right = step(
        block_slot, refresh_list, activations, out_grad,
        left_factor[0, 0], right_factor[0, 0], left_root[0, 0], right_root[0, 0],
    )
    direction, new_left, new_right = arrange(block_slot, every, new_left, new_right)
    return (direction, new_left[None, None], new_right[None, None])


def solution(mesh):
    in_specs = (
        P("dp", "mp"),
        P("dp", "mp"),
        P(),
        P(),
        P("dp", "mp", None, None),
        P("dp", "mp", None, None),
        P("dp", "mp", None, None),
        P("dp", "mp", None, None),
    )
    out_specs = (P(None, "mp"), P("dp", "mp", None, None), P("dp", "mp", None, None))
    return jax.shard_map(body, mesh=mesh, in_specs=in_specs, out_specs=out_specs, check_vma=False)
```

```python
import jax
import jax.numpy as jnp
from jax import lax
from jax.experimental import pallas as pl
from jax.experimental.pallas import tpu as pltpu
from jax.sharding import PartitionSpec as P

NZ, NX, NY = 8, 4, 4
SIDE = 512
FEAT = 64
A_ROWS = 288
HALF = A_ROWS // 2
MESH = pl.DeviceIdType.MESH
VMEM_LIMIT = 40 * 1024 * 1024


def place():
    dp, mp = lax.axis_index("dp"), lax.axis_index("mp")
    return dp // 2, dp % 2, mp // 8, (mp // 2) % 4, mp % 2


def device(z, h, l, x, k):
    return (2 * z + h, 8 * l + 2 * x + k)


def inverse_roots(statistics):
    shape = statistics[0].shape
    rows = lax.broadcasted_iota(jnp.int32, shape, 0)
    cols = lax.broadcasted_iota(jnp.int32, shape, 1)
    identity = jnp.where(rows == cols, 1.0, 0.0).astype(jnp.float32)

    def dot(left, right):
        return jnp.dot(left, right, preferred_element_type=jnp.float32)

    def half(values):
        return [v.astype(jnp.bfloat16) for v in values]

    def next_dev(dev, narrow):
        square = half([dot(n, n) + (1.5625 * identity - 2.5 * e) for e, n in zip(dev, narrow)])
        fourth = half([dot(f, f) for f in square])
        return [dot(f, n) for f, n in zip(fourth, narrow)]

    scaling = [2.5 / jnp.sqrt(jnp.sum(a * a)) for a in statistics]
    first = [a * (0.25 * c) for a, c in zip(statistics, scaling)]
    first_n = half(first)
    second = next_dev(first, first_n)
    second_n = half(second)
    pair = [1.25 * (e + f) - dot(m, n) for e, f, m, n in zip(first, second, first_n, second_n)]
    third = next_dev(second, second_n)
    result = [
        1.953125 * identity - 1.25 * p - 1.5625 * e + dot(m, n)
        for p, e, m, n in zip(pair, third, half(pair), half(third))
    ]
    return [(x * jnp.sqrt(jnp.sqrt(c))).astype(jnp.bfloat16) for x, c in zip(result, scaling)]


def step_kernel(
    slots_hbm, refresh_hbm, act_hbm, out_hbm, lf_hbm, rf_hbm, lr_hbm, rr_hbm, every, nl_ref, nr_ref,
    slots_ref, refresh_ref, act_ref, out_ref, lf_ref, rf_ref, lr_ref, rr_ref, load_s, cot, act, flipped, total, table, outgoing, tile,
    swap_s, swap_r, ring_s, ring_r, turn_s, turn_r, plane_s, plane_r,
    pass_s, pass_r, give_s, give_r, local_s, z_s, z_r, zb_s, zb_r, y_s, y_r, yb_s, yb_r,
):
    z, h, l, x, k = place()
    dp, mp = lax.axis_index("dp"), lax.axis_index("mp")
    y = 2 * h + l
    up, down = (z + 1) % NZ, (z + NZ - 1) % NZ

    loads = [
        pltpu.make_async_copy(src, dst, load_s.at[i])
        for i, (src, dst) in enumerate(
            (
                (act_hbm, act_ref), (out_hbm, out_ref), (slots_hbm, slots_ref), (refresh_hbm, refresh_ref),
                (lf_hbm, lf_ref), (rf_hbm, rf_ref), (lr_hbm, lr_ref), (rr_hbm, rr_ref),
            )
        )
    ]
    for copy in loads:
        copy.start()
    barrier = pltpu.get_barrier_semaphore()

    def x_peer(step):
        return device(z, h, l, (x + step) % NX, k)

    def y_peer(step):
        there = (y + step) % NY
        return device(z, there // 2, there % 2, x, k)

    def greet(target):
        pl.semaphore_signal(barrier, inc=1, device_id=target, device_id_type=MESH)

    greet(device(up, h, l, x, k))
    greet(device(down, h, l, x, k))
    for step in range(1, 4):
        greet(x_peer(step))
        greet(y_peer(step))
    for i in range(4):
        source = 2 * i + k

        @pl.when(jnp.logical_not(jnp.logical_and(source == z, z // 4 == k)))
        def _():
            greet(device(source, h, l, x, z // 4))

    loads[1].wait()
    for c in range(2):
        cot[z, pl.ds(h * 128, 128), c * 256 : c * 256 + 256] = out_ref[
            :, pl.ds(pl.multiple_of(c * 512 + 256 * h, 256), 256)
        ]
    pl.semaphore_wait(barrier, 12 - jnp.where(jnp.logical_and(z // 4 == k, z % 2 == k), 1, 0))

    def send(src, dst, ssem, rsem, target):
        copy = pltpu.make_async_remote_copy(
            src_ref=src, dst_ref=dst, send_sem=ssem, recv_sem=rsem, device_id=target, device_id_type=MESH
        )
        copy.start()
        return copy

    pending = []

    for c in range(2):
        pending.append(
            send(
                out_ref.at[:, pl.ds(pl.multiple_of(c * 512 + 256 * (1 - h), 256), 256)],
                cot.at[z, pl.ds(pl.multiple_of(h * 128, 128), 128), pl.ds(c * 256, 256)],
                swap_s.at[c], swap_r.at[c], (2 * z + 1 - h, mp),
            )
        )

    def unit(source, u):
        return cot.at[source, pl.ds(pl.multiple_of(u * 128, 128), 128), :]

    def ring(direction, step, u):
        source = (z + NZ - step) % NZ if direction == 0 else (z + step) % NZ
        target = up if direction == 0 else down
        view = unit(source, u)
        pending.append(
            send(view, view, ring_s.at[direction, step, u], ring_r.at[direction, step, u], (2 * target + h, mp))
        )

    def ring_wait(direction, step, u):
        source = (z + NZ - step) % NZ if direction == 0 else (z + step) % NZ
        view = unit(source, u)
        pltpu.make_async_remote_copy(
            src_ref=view, dst_ref=view, send_sem=ring_s.at[direction, step - 1, u],
            recv_sem=ring_r.at[direction, step - 1, u], device_id=(dp, mp), device_id_type=MESH,
        ).wait_recv()

    ring(0, 0, h)
    ring(1, 0, h)


    loads[0].wait()
    flipped[...] = act_ref[...].astype(jnp.float32).T.astype(jnp.bfloat16)

    def turn_view(source):
        return act.at[source // 2, source % 2, l, x, :, pl.ds(pl.multiple_of(h * 128, 128), 128)]

    for j in range(4):
        target = 4 * k + j
        here = jnp.logical_and(target == z, z % 2 == k)
        src = flipped.at[j * FEAT : (j + 1) * FEAT, :]

        @pl.when(jnp.logical_not(here))
        def _():
            send(src, turn_view(z), turn_s.at[j], turn_r.at[z], device(target, h, l, x, z % 2))

        @pl.when(here)
        def _():
            pltpu.make_async_copy(src, turn_view(z), turn_r.at[z]).start()

    for c in range(2):
        view = cot.at[z, pl.ds(pl.multiple_of((1 - h) * 128, 128), 128), pl.ds(c * 256, 256)]
        pltpu.make_async_copy(view, view, swap_r.at[c]).wait()
    ring(0, 0, 1 - h)
    ring(1, 0, 1 - h)

    for i in range(4):
        source = 2 * i + k
        view = turn_view(source)
        pltpu.make_async_copy(view, view, turn_r.at[source]).wait()

    def tokens(half):
        return pl.ds(pl.multiple_of(half * 128, 128), 128)

    def first_view(part, col, row):
        return act.at[2 * part : 2 * part + 2, k, row % 2, col, :, tokens(row // 2)]

    def second_view(part, index):
        if part == 0:
            return act.at[0:2, k, index % 2, :, :, tokens(index // 2)]
        return act.at[2:4, k, :, index]

    def peer(axis, step):
        return x_peer(step) if axis == 0 else y_peer(step)

    def back(axis, step):
        return (x + NX - step) % NX if axis == 0 else (y + NY - step) % NY

    for step in (1, 2, 3):
        for part in (0, 1):
            view = first_view(part, x, y)
            pending.append(send(view, view, plane_s.at[0, part, step], plane_r.at[0, part, step], peer(part, step)))

    def advance(step):
        for u in (h, 1 - h):
            for direction in (0, 1):
                ring_wait(direction, step, u)
                ring(direction, step, u)

    advance(1)
    for part in (0, 1):
        for step in (1, 2, 3):
            view = first_view(0, back(0, step), y) if part == 0 else first_view(1, x, back(1, step))
            pltpu.make_async_copy(view, view, plane_r.at[0, part, step]).wait()
        view = second_view(part, y if part == 0 else x)
        for step in (1, 2, 3):
            pending.append(
                send(view, view, plane_s.at[1, part, step], plane_r.at[1, part, step], peer(1 - part, step))
            )
    advance(2)

    for part in (0, 1):
        for step in (1, 2, 3):
            view = second_view(part, back(1 - part, step))
            pltpu.make_async_copy(view, view, plane_r.at[1, part, step]).wait()
        view = act.at[2 * part : 2 * part + 2, k]
        pending.append(send(view, view, pass_s.at[part], pass_r.at[part], device(z, h, l, x, 1 - k)))

    def held(slot):
        found = jnp.int32(0)
        for b in range(16):
            found = jnp.maximum(found, jnp.where(slots_ref[mp, b] == slot, b, 0))
        return found

    loads[2].wait()
    loads[3].wait()
    for slot in range(16):
        table[slot] = held(slot)

    for u in (h, 1 - h):
        for direction in (0, 1):
            ring_wait(direction, 3, u)
    ring(0, 3, 0)
    ring(1, 3, 1)

    for part in (0, 1):
        view = act.at[2 * part : 2 * part + 2, 1 - k]
        pltpu.make_async_copy(view, view, pass_r.at[part]).wait()

    def product(source):
        return jnp.dot(
            act[source // 2, source % 2].reshape(8 * FEAT, 256), cot[source], preferred_element_type=jnp.float32
        )

    def add(value):
        for c in range(2):
            total[:, c] += value[:, c * 256 : (c + 1) * 256].reshape(8, FEAT, 256)

    total[...] = jnp.zeros_like(total)
    add(product(z))

    @pl.loop(1, 4)
    def _(step):
        add(product((z + step) % NZ) + product((z + NZ - step) % NZ))

    ring_wait(0, 4, 0)
    ring_wait(1, 4, 1)
    add(product((z + 4) % NZ))

    def piece(slot):
        block = table[slot]
        return total[block // 2, block % 2].astype(jnp.bfloat16)

    def spot(slot):
        return tile.at[
            pl.ds(pl.multiple_of((slot // 2) * FEAT, FEAT), FEAT), pl.ds(pl.multiple_of((slot % 2) * 256, 256), 256)
        ]

    for dz in (4, 3, 5, 2, 6, 1, 7, 0):
        for dh in (0, 1):
            if (dz, dh) != (0, 0):
                slot = 2 * ((z + dz) % NZ) + (h + dh) % 2
                outgoing[slot] = piece(slot)
                send(outgoing.at[slot], spot(dp), give_s.at[slot], give_r.at[dp], (slot, mp))

    outgoing[dp] = piece(dp)
    own = pltpu.make_async_copy(outgoing.at[dp], spot(dp), local_s)
    own.start()
    own.wait()

    @pl.loop(1, 16)
    def _(step):
        slot = (dp + step) % 16
        view = spot(slot)
        pltpu.make_async_copy(view, view, give_r.at[slot]).wait()

    for copy in loads[4:]:
        copy.wait()
    mine = table[dp]
    hits = jnp.int32(0)
    for j in range(4):
        hits += jnp.where(refresh_ref[j, mp] == mine, 1, 0)
    chosen = jnp.broadcast_to(hits > 0, (SIDE, SIDE))
    grad = tile[...]
    left = lax.dot_general(grad, grad, (((1,), (1,)), ((), ())), preferred_element_type=jnp.float32)
    right = lax.dot_general(grad, grad, (((0,), (0,)), ((), ())), preferred_element_type=jnp.float32)
    lroot, rroot = inverse_roots((0.9 * lf_ref[...] + left, 0.9 * rf_ref[...] + right))
    nl_ref[...] = jnp.where(chosen, lroot, lr_ref[...])
    nr_ref[...] = jnp.where(chosen, rroot, rr_ref[...])
    mixed = jnp.dot(nl_ref[...], grad, preferred_element_type=jnp.float32).astype(jnp.bfloat16)
    precond = jnp.dot(mixed, nr_ref[...], preferred_element_type=jnp.float32)
    wide = grad.astype(jnp.float32)
    ratio = jnp.sqrt((jnp.sum(wide * wide) + 1e-06) / (jnp.sum(precond * precond) + 1e-06))
    every[dp] = (precond * ratio).astype(jnp.bfloat16)

    ends = ((2 * up + h, mp), (2 * down + h, mp))
    partner = (2 * z + 1 - h, mp)

    def arrived(view, sem):
        pltpu.make_async_copy(view, view, sem).wait()

    def source(direction, step):
        return (z + NZ - step) % NZ if direction == 0 else (z + step) % NZ

    def a_rows(direction, step):
        if step < 3:
            return pl.ds(0, A_ROWS)
        return pl.ds(direction * HALF, HALF)

    def post(src, dst, ssem, rsem, target):
        pending.append(send(src, dst, ssem, rsem, target))

    def a_view(slot, rows):
        return every.at[slot, rows, :]

    def b_view(slot):
        return every.at[slot, pl.ds(A_ROWS, SIDE - A_ROWS), :]

    def z_a(direction, step):
        rows = a_rows(direction, step)
        dst = a_view(2 * source(direction, step) + h, rows)
        src = dst
        post(src, dst, z_s.at[direction, step], z_r.at[direction, step], ends[direction])

    def z_b(direction, step, u):
        dst = b_view(2 * source(direction, step) + u)
        src = dst
        post(src, dst, zb_s.at[direction, step, u], zb_r.at[direction, step, u], ends[direction])

    def y_a(index, slot, rows):
        dst = a_view(slot, rows)
        post(dst, dst, y_s.at[index], y_r.at[index], partner)

    full = pl.ds(0, A_ROWS)
    z_a(0, 0)
    z_a(1, 0)
    post(b_view(dp), b_view(dp), yb_s, yb_r, partner)
    y_a(0, dp, full)
    z_b(0, 0, h)
    z_b(1, 0, h)
    arrived(b_view(2 * z + 1 - h), yb_r)
    z_b(0, 0, 1 - h)
    z_b(1, 0, 1 - h)

    for step in (1, 2, 3):
        for direction in (0, 1):
            slot = 2 * source(direction, step) + h
            arrived(a_view(slot, full), z_r.at[direction, step - 1])
            z_a(direction, step)
            y_a(1 + 3 * direction + step - 1, slot, full)
        for u in (h, 1 - h):
            for direction in (0, 1):
                arrived(b_view(2 * source(direction, step) + u), zb_r.at[direction, step - 1, u])
                if step < 3:
                    z_b(direction, step, u)
        if step == 3:
            z_b(0, 3, 0)
            z_b(1, 3, 1)
    for direction in (0, 1):
        rows = a_rows(direction, 3)
        slot = 2 * source(direction, 4) + h
        arrived(a_view(slot, rows), z_r.at[direction, 3])
        y_a(7 + direction, slot, rows)
    arrived(b_view(2 * source(0, 4)), zb_r.at[0, 3, 0])
    arrived(b_view(2 * source(1, 4) + 1), zb_r.at[1, 3, 1])

    other = 1 - h
    arrived(a_view(2 * z + other, full), y_r.at[0])
    for direction in (0, 1):
        for step in (1, 2, 3):
            arrived(a_view(2 * source(direction, step) + other, full), y_r.at[1 + 3 * direction + step - 1])
    for direction in (0, 1):
        arrived(a_view(2 * source(direction, 4) + other, a_rows(direction, 3)), y_r.at[7 + direction])

    for copy in pending:
        copy.wait_send()

    @pl.loop(1, 16)
    def _(step):
        slot = (dp + step) % 16
        pltpu.make_async_copy(outgoing.at[slot], outgoing.at[slot], give_s.at[slot]).wait()

    for j in range(4):
        here = jnp.logical_and(4 * k + j == z, z % 2 == k)
        src = flipped.at[j * FEAT : (j + 1) * FEAT, :]

        @pl.when(jnp.logical_not(here))
        def _():
            pltpu.make_async_copy(src, src, turn_s.at[j]).wait()


def step(block_slot, refresh_list, activations, out_grad, left_factor, right_factor, left_root, right_root):
    dma = pltpu.SemaphoreType.DMA
    vmem = pl.BlockSpec(memory_space=pltpu.VMEM)
    tile = jax.ShapeDtypeStruct((SIDE, SIDE), jnp.bfloat16)
    return pl.pallas_call(
        step_kernel,
        name="step",
        out_shape=(jax.ShapeDtypeStruct((16, SIDE, SIDE), jnp.bfloat16), tile, tile),
        in_specs=[pl.BlockSpec(memory_space=pltpu.HBM)] * 8,
        out_specs=(vmem, vmem, vmem),
        scratch_shapes=[
            pltpu.SMEM((16, 16), jnp.int32),
            pltpu.SMEM((4, 16), jnp.int32),
            pltpu.VMEM((128, 256), jnp.bfloat16),
            pltpu.VMEM((128, 1024), jnp.bfloat16),
            pltpu.VMEM((SIDE, SIDE), jnp.float32),
            pltpu.VMEM((SIDE, SIDE), jnp.float32),
            pltpu.VMEM((SIDE, SIDE), jnp.bfloat16),
            pltpu.VMEM((SIDE, SIDE), jnp.bfloat16),
            dma((8,)),
            pltpu.VMEM((NZ, 256, SIDE), jnp.bfloat16),
            pltpu.VMEM((4, 2, 2, NX, FEAT, 256), jnp.bfloat16),
            pltpu.VMEM((256, 128), jnp.bfloat16),
            pltpu.VMEM((8, 2, FEAT, 256), jnp.float32),
            pltpu.SMEM((16,), jnp.int32),
            pltpu.VMEM((16, FEAT, 256), jnp.bfloat16),
            pltpu.VMEM((SIDE, SIDE), jnp.bfloat16),
            dma((2,)), dma((2,)), dma((2, 4, 2)), dma((2, 4, 2)), dma((4,)), dma((NZ,)), dma((2, 2, 4)), dma((2, 2, 4)),
            dma((2,)), dma((2,)), dma((16,)), dma((16,)), dma,
            dma((2, 4)), dma((2, 4)), dma((2, 4, 2)), dma((2, 4, 2)), dma((9,)), dma((9,)), dma, dma,
        ],
        compiler_params=pltpu.CompilerParams(collective_id=1, has_side_effects=True, vmem_limit_bytes=VMEM_LIMIT),
        cost_estimate=pl.CostEstimate(flops=2 * 512**3 * 24, bytes_accessed=20 << 20, transcendentals=0),
    )(*(
        pltpu.with_memory_space_constraint(x, pltpu.HBM)
        for x in (block_slot, refresh_list.T, activations, out_grad, left_factor, right_factor, left_root, right_root)
    ))


def arrange_kernel(slots_hbm, every, left, right, out_hbm, nl_hbm, nr_hbm, slots_ref, sem):
    mp = lax.axis_index("mp")
    load = pltpu.make_async_copy(slots_hbm, slots_ref, sem.at[16])
    load.start()
    copies = [
        pltpu.make_async_copy(left, nl_hbm, sem.at[17]),
        pltpu.make_async_copy(right, nr_hbm, sem.at[18]),
    ]
    for copy in copies:
        copy.start()
    load.wait()
    for b in range(16):
        copy = pltpu.make_async_copy(
            every.at[slots_ref[mp, b]],
            out_hbm.at[pl.ds((b // 2) * SIDE, SIDE), pl.ds((b % 2) * SIDE, SIDE)],
            sem.at[b],
        )
        copy.start()
        copies.append(copy)
    for copy in copies:
        copy.wait()


def arrange(block_slot, every, left, right):
    hbm = pl.BlockSpec(memory_space=pltpu.HBM)
    vmem = pl.BlockSpec(memory_space=pltpu.VMEM)
    tile = jax.ShapeDtypeStruct((SIDE, SIDE), jnp.bfloat16)
    return pl.pallas_call(
        arrange_kernel,
        name="arrange",
        in_specs=[hbm, vmem, vmem, vmem],
        out_specs=(hbm, hbm, hbm),
        out_shape=(jax.ShapeDtypeStruct((8 * SIDE, 2 * SIDE), jnp.bfloat16), tile, tile),
        scratch_shapes=[pltpu.SMEM((16, 16), jnp.int32), pltpu.SemaphoreType.DMA((19,))],
        compiler_params=pltpu.CompilerParams(vmem_limit_bytes=VMEM_LIMIT),
        cost_estimate=pl.CostEstimate(flops=0, bytes_accessed=16 << 20, transcendentals=0),
    )(pltpu.with_memory_space_constraint(block_slot, pltpu.HBM), every, left, right)


def body(
    activations,
    out_grad,
    block_slot,
    refresh_list,
    left_factor,
    right_factor,
    left_root,
    right_root,
):
    every, new_left, new_right = step(
        block_slot, refresh_list, activations, out_grad,
        left_factor[0, 0], right_factor[0, 0], left_root[0, 0], right_root[0, 0],
    )
    direction, new_left, new_right = arrange(block_slot, every, new_left, new_right)
    return (direction, new_left[None, None], new_right[None, None])


def solution(mesh):
    in_specs = (
        P("dp", "mp"),
        P("dp", "mp"),
        P(),
        P(),
        P("dp", "mp", None, None),
        P("dp", "mp", None, None),
        P("dp", "mp", None, None),
        P("dp", "mp", None, None),
    )
    out_specs = (P(None, "mp"), P("dp", "mp", None, None), P("dp", "mp", None, None))
    return jax.shard_map(body, mesh=mesh, in_specs=in_specs, out_specs=out_specs, check_vma=False)
```

```python
import jax
import jax.numpy as jnp
from jax import lax
from jax.experimental import pallas as pl
from jax.experimental.pallas import tpu as pltpu
from jax.sharding import PartitionSpec as P

NZ, NX, NY = 8, 4, 4
SIDE = 512
FEAT = 64
A_ROWS = 288
HALF = A_ROWS // 2
MESH = pl.DeviceIdType.MESH
VMEM_LIMIT = 40 * 1024 * 1024


def place():
    dp, mp = lax.axis_index("dp"), lax.axis_index("mp")
    return dp // 2, dp % 2, mp // 8, (mp // 2) % 4, mp % 2


def device(z, h, l, x, k):
    return (2 * z + h, 8 * l + 2 * x + k)


def inverse_roots(statistics):
    shape = statistics[0].shape
    rows = lax.broadcasted_iota(jnp.int32, shape, 0)
    cols = lax.broadcasted_iota(jnp.int32, shape, 1)
    identity = jnp.where(rows == cols, 1.0, 0.0).astype(jnp.float32)

    def dot(left, right):
        return jnp.dot(left, right, preferred_element_type=jnp.float32)

    def parts(value, wide):
        high = value.astype(jnp.bfloat16)
        return (high, (value - high.astype(jnp.float32)).astype(jnp.bfloat16)) if wide else (high,)

    def product(left, right):
        total = dot(left[0], right[0])
        if len(left) == 2:
            total += dot(left[0], right[1]) + dot(left[1], right[0])
        return total

    def next_dev(dev, wide):
        narrow = [parts(e, wide) for e in dev]
        d = [2.5 * e - product(n, n) for e, n in zip(dev, narrow)]
        d_n = [parts(x, wide) for x in d]
        h = [parts(3.125 * x - product(n, n), wide) for x, n in zip(d, d_n)]
        return [2.44140625 * e - product(x, n) for e, x, n in zip(dev, h, narrow)]

    def plain(left, right):
        return dot(left.astype(jnp.bfloat16), right.astype(jnp.bfloat16))

    scaling = [2.5 / jnp.sqrt(jnp.sum(a * a)) for a in statistics]
    first = [a * (0.25 * c) for a, c in zip(statistics, scaling)]
    second = next_dev(first, True)
    third = next_dev(second, False)
    pair = [1.25 * (e + f) - plain(e, f) for e, f in zip(first, second)]
    result = [1.953125 * identity - 1.25 * p - 1.5625 * e + plain(p, e) for p, e in zip(pair, third)]
    return [(x * jnp.sqrt(jnp.sqrt(c))).astype(jnp.bfloat16) for x, c in zip(result, scaling)]


def step_kernel(
    slots_hbm, refresh_hbm, act_hbm, out_hbm, lf_hbm, rf_hbm, lr_hbm, rr_hbm, every, nl_ref, nr_ref,
    slots_ref, refresh_ref, act_ref, out_ref, lf_ref, rf_ref, lr_ref, rr_ref, load_s, cot, act, flipped, total, table, outgoing, tile,
    swap_s, swap_r, ring_s, ring_r, turn_s, turn_r, plane_s, plane_r,
    pass_s, pass_r, give_s, give_r, local_s, z_s, z_r, zb_s, zb_r, y_s, y_r, yb_s, yb_r,
):
    z, h, l, x, k = place()
    dp, mp = lax.axis_index("dp"), lax.axis_index("mp")
    y = 2 * h + l
    up, down = (z + 1) % NZ, (z + NZ - 1) % NZ

    loads = [
        pltpu.make_async_copy(src, dst, load_s.at[i])
        for i, (src, dst) in enumerate(
            (
                (act_hbm, act_ref), (out_hbm, out_ref), (slots_hbm, slots_ref), (refresh_hbm, refresh_ref),
                (lf_hbm, lf_ref), (rf_hbm, rf_ref), (lr_hbm, lr_ref), (rr_hbm, rr_ref),
            )
        )
    ]
    for copy in loads:
        copy.start()
    barrier = pltpu.get_barrier_semaphore()

    def x_peer(step):
        return device(z, h, l, (x + step) % NX, k)

    def y_peer(step):
        there = (y + step) % NY
        return device(z, there // 2, there % 2, x, k)

    def greet(target):
        pl.semaphore_signal(barrier, inc=1, device_id=target, device_id_type=MESH)

    greet(device(up, h, l, x, k))
    greet(device(down, h, l, x, k))
    for step in range(1, 4):
        greet(x_peer(step))
        greet(y_peer(step))
    for i in range(4):
        source = 2 * i + k

        @pl.when(jnp.logical_not(jnp.logical_and(source == z, z // 4 == k)))
        def _():
            greet(device(source, h, l, x, z // 4))

    loads[1].wait()
    for c in range(2):
        cot[z, pl.ds(h * 128, 128), c * 256 : c * 256 + 256] = out_ref[
            :, pl.ds(pl.multiple_of(c * 512 + 256 * h, 256), 256)
        ]
    pl.semaphore_wait(barrier, 12 - jnp.where(jnp.logical_and(z // 4 == k, z % 2 == k), 1, 0))

    def send(src, dst, ssem, rsem, target):
        copy = pltpu.make_async_remote_copy(
            src_ref=src, dst_ref=dst, send_sem=ssem, recv_sem=rsem, device_id=target, device_id_type=MESH
        )
        copy.start()
        return copy

    pending = []

    for c in range(2):
        pending.append(
            send(
                out_ref.at[:, pl.ds(pl.multiple_of(c * 512 + 256 * (1 - h), 256), 256)],
                cot.at[z, pl.ds(pl.multiple_of(h * 128, 128), 128), pl.ds(c * 256, 256)],
                swap_s.at[c], swap_r.at[c], (2 * z + 1 - h, mp),
            )
        )

    def unit(source, u):
        return cot.at[source, pl.ds(pl.multiple_of(u * 128, 128), 128), :]

    def ring(direction, step, u):
        source = (z + NZ - step) % NZ if direction == 0 else (z + step) % NZ
        target = up if direction == 0 else down
        view = unit(source, u)
        pending.append(
            send(view, view, ring_s.at[direction, step, u], ring_r.at[direction, step, u], (2 * target + h, mp))
        )

    def ring_wait(direction, step, u):
        source = (z + NZ - step) % NZ if direction == 0 else (z + step) % NZ
        view = unit(source, u)
        pltpu.make_async_remote_copy(
            src_ref=view, dst_ref=view, send_sem=ring_s.at[direction, step - 1, u],
            recv_sem=ring_r.at[direction, step - 1, u], device_id=(dp, mp), device_id_type=MESH,
        ).wait_recv()

    ring(0, 0, h)
    ring(1, 0, h)


    loads[0].wait()
    flipped[...] = act_ref[...].astype(jnp.float32).T.astype(jnp.bfloat16)

    def turn_view(source):
        return act.at[source // 2, source % 2, l, x, :, pl.ds(pl.multiple_of(h * 128, 128), 128)]

    for j in range(4):
        target = 4 * k + j
        here = jnp.logical_and(target == z, z % 2 == k)
        src = flipped.at[j * FEAT : (j + 1) * FEAT, :]

        @pl.when(jnp.logical_not(here))
        def _():
            send(src, turn_view(z), turn_s.at[j], turn_r.at[z], device(target, h, l, x, z % 2))

        @pl.when(here)
        def _():
            pltpu.make_async_copy(src, turn_view(z), turn_r.at[z]).start()

    for c in range(2):
        view = cot.at[z, pl.ds(pl.multiple_of((1 - h) * 128, 128), 128), pl.ds(c * 256, 256)]
        pltpu.make_async_copy(view, view, swap_r.at[c]).wait()
    ring(0, 0, 1 - h)
    ring(1, 0, 1 - h)

    for i in range(4):
        source = 2 * i + k
        view = turn_view(source)
        pltpu.make_async_copy(view, view, turn_r.at[source]).wait()

    def tokens(half):
        return pl.ds(pl.multiple_of(half * 128, 128), 128)

    def first_view(part, col, row):
        return act.at[2 * part : 2 * part + 2, k, row % 2, col, :, tokens(row // 2)]

    def second_view(part, index):
        if part == 0:
            return act.at[0:2, k, index % 2, :, :, tokens(index // 2)]
        return act.at[2:4, k, :, index]

    def peer(axis, step):
        return x_peer(step) if axis == 0 else y_peer(step)

    def back(axis, step):
        return (x + NX - step) % NX if axis == 0 else (y + NY - step) % NY

    for step in (1, 2, 3):
        for part in (0, 1):
            view = first_view(part, x, y)
            pending.append(send(view, view, plane_s.at[0, part, step], plane_r.at[0, part, step], peer(part, step)))

    def advance(step):
        for u in (h, 1 - h):
            for direction in (0, 1):
                ring_wait(direction, step, u)
                ring(direction, step, u)

    advance(1)
    for part in (0, 1):
        for step in (1, 2, 3):
            view = first_view(0, back(0, step), y) if part == 0 else first_view(1, x, back(1, step))
            pltpu.make_async_copy(view, view, plane_r.at[0, part, step]).wait()
        view = second_view(part, y if part == 0 else x)
        for step in (1, 2, 3):
            pending.append(
                send(view, view, plane_s.at[1, part, step], plane_r.at[1, part, step], peer(1 - part, step))
            )
    advance(2)

    for part in (0, 1):
        for step in (1, 2, 3):
            view = second_view(part, back(1 - part, step))
            pltpu.make_async_copy(view, view, plane_r.at[1, part, step]).wait()
        view = act.at[2 * part : 2 * part + 2, k]
        pending.append(send(view, view, pass_s.at[part], pass_r.at[part], device(z, h, l, x, 1 - k)))

    def held(slot):
        found = jnp.int32(0)
        for b in range(16):
            found = jnp.maximum(found, jnp.where(slots_ref[mp, b] == slot, b, 0))
        return found

    loads[2].wait()
    loads[3].wait()
    for slot in range(16):
        table[slot] = held(slot)

    for u in (h, 1 - h):
        for direction in (0, 1):
            ring_wait(direction, 3, u)
    ring(0, 3, 0)
    ring(1, 3, 1)

    for part in (0, 1):
        view = act.at[2 * part : 2 * part + 2, 1 - k]
        pltpu.make_async_copy(view, view, pass_r.at[part]).wait()

    def product(source):
        return jnp.dot(
            act[source // 2, source % 2].reshape(8 * FEAT, 256), cot[source], preferred_element_type=jnp.float32
        )

    def add(value):
        for c in range(2):
            total[:, c] += value[:, c * 256 : (c + 1) * 256].reshape(8, FEAT, 256)

    total[...] = jnp.zeros_like(total)
    add(product(z))

    @pl.loop(1, 4)
    def _(step):
        add(product((z + step) % NZ) + product((z + NZ - step) % NZ))

    ring_wait(0, 4, 0)
    ring_wait(1, 4, 1)
    add(product((z + 4) % NZ))

    def piece(slot):
        block = table[slot]
        return total[block // 2, block % 2].astype(jnp.bfloat16)

    def spot(slot):
        return tile.at[
            pl.ds(pl.multiple_of((slot // 2) * FEAT, FEAT), FEAT), pl.ds(pl.multiple_of((slot % 2) * 256, 256), 256)
        ]

    for dz in (4, 3, 5, 2, 6, 1, 7, 0):
        for dh in (0, 1):
            if (dz, dh) != (0, 0):
                slot = 2 * ((z + dz) % NZ) + (h + dh) % 2
                outgoing[slot] = piece(slot)
                send(outgoing.at[slot], spot(dp), give_s.at[slot], give_r.at[dp], (slot, mp))

    outgoing[dp] = piece(dp)
    own = pltpu.make_async_copy(outgoing.at[dp], spot(dp), local_s)
    own.start()
    own.wait()

    @pl.loop(1, 16)
    def _(step):
        slot = (dp + step) % 16
        view = spot(slot)
        pltpu.make_async_copy(view, view, give_r.at[slot]).wait()

    for copy in loads[4:]:
        copy.wait()
    mine = table[dp]
    hits = jnp.int32(0)
    for j in range(4):
        hits += jnp.where(refresh_ref[j, mp] == mine, 1, 0)
    chosen = jnp.broadcast_to(hits > 0, (SIDE, SIDE))
    grad = tile[...]
    left = lax.dot_general(grad, grad, (((1,), (1,)), ((), ())), preferred_element_type=jnp.float32)
    right = lax.dot_general(grad, grad, (((0,), (0,)), ((), ())), preferred_element_type=jnp.float32)
    lroot, rroot = inverse_roots((0.9 * lf_ref[...] + left, 0.9 * rf_ref[...] + right))
    nl_ref[...] = jnp.where(chosen, lroot, lr_ref[...])
    nr_ref[...] = jnp.where(chosen, rroot, rr_ref[...])
    mixed = jnp.dot(nl_ref[...], grad, preferred_element_type=jnp.float32).astype(jnp.bfloat16)
    precond = jnp.dot(mixed, nr_ref[...], preferred_element_type=jnp.float32)
    wide = grad.astype(jnp.float32)
    ratio = jnp.sqrt((jnp.sum(wide * wide) + 1e-06) / (jnp.sum(precond * precond) + 1e-06))
    every[dp] = (precond * ratio).astype(jnp.bfloat16)

    ends = ((2 * up + h, mp), (2 * down + h, mp))
    partner = (2 * z + 1 - h, mp)

    def arrived(view, sem):
        pltpu.make_async_copy(view, view, sem).wait()

    def source(direction, step):
        return (z + NZ - step) % NZ if direction == 0 else (z + step) % NZ

    def a_rows(direction, step):
        if step < 3:
            return pl.ds(0, A_ROWS)
        return pl.ds(direction * HALF, HALF)

    def post(src, dst, ssem, rsem, target):
        pending.append(send(src, dst, ssem, rsem, target))

    def a_view(slot, rows):
        return every.at[slot, rows, :]

    def b_view(slot):
        return every.at[slot, pl.ds(A_ROWS, SIDE - A_ROWS), :]

    def z_a(direction, step):
        rows = a_rows(direction, step)
        dst = a_view(2 * source(direction, step) + h, rows)
        src = dst
        post(src, dst, z_s.at[direction, step], z_r.at[direction, step], ends[direction])

    def z_b(direction, step, u):
        dst = b_view(2 * source(direction, step) + u)
        src = dst
        post(src, dst, zb_s.at[direction, step, u], zb_r.at[direction, step, u], ends[direction])

    def y_a(index, slot, rows):
        dst = a_view(slot, rows)
        post(dst, dst, y_s.at[index], y_r.at[index], partner)

    full = pl.ds(0, A_ROWS)
    z_a(0, 0)
    z_a(1, 0)
    post(b_view(dp), b_view(dp), yb_s, yb_r, partner)
    y_a(0, dp, full)
    z_b(0, 0, h)
    z_b(1, 0, h)
    arrived(b_view(2 * z + 1 - h), yb_r)
    z_b(0, 0, 1 - h)
    z_b(1, 0, 1 - h)

    for step in (1, 2, 3):
        for direction in (0, 1):
            slot = 2 * source(direction, step) + h
            arrived(a_view(slot, full), z_r.at[direction, step - 1])
            z_a(direction, step)
            y_a(1 + 3 * direction + step - 1, slot, full)
        for u in (h, 1 - h):
            for direction in (0, 1):
                arrived(b_view(2 * source(direction, step) + u), zb_r.at[direction, step - 1, u])
                if step < 3:
                    z_b(direction, step, u)
        if step == 3:
            z_b(0, 3, 0)
            z_b(1, 3, 1)
    for direction in (0, 1):
        rows = a_rows(direction, 3)
        slot = 2 * source(direction, 4) + h
        arrived(a_view(slot, rows), z_r.at[direction, 3])
        y_a(7 + direction, slot, rows)
    arrived(b_view(2 * source(0, 4)), zb_r.at[0, 3, 0])
    arrived(b_view(2 * source(1, 4) + 1), zb_r.at[1, 3, 1])

    other = 1 - h
    arrived(a_view(2 * z + other, full), y_r.at[0])
    for direction in (0, 1):
        for step in (1, 2, 3):
            arrived(a_view(2 * source(direction, step) + other, full), y_r.at[1 + 3 * direction + step - 1])
    for direction in (0, 1):
        arrived(a_view(2 * source(direction, 4) + other, a_rows(direction, 3)), y_r.at[7 + direction])

    for copy in pending:
        copy.wait_send()

    @pl.loop(1, 16)
    def _(step):
        slot = (dp + step) % 16
        pltpu.make_async_copy(outgoing.at[slot], outgoing.at[slot], give_s.at[slot]).wait()

    for j in range(4):
        here = jnp.logical_and(4 * k + j == z, z % 2 == k)
        src = flipped.at[j * FEAT : (j + 1) * FEAT, :]

        @pl.when(jnp.logical_not(here))
        def _():
            pltpu.make_async_copy(src, src, turn_s.at[j]).wait()


def step(block_slot, refresh_list, activations, out_grad, left_factor, right_factor, left_root, right_root):
    dma = pltpu.SemaphoreType.DMA
    vmem = pl.BlockSpec(memory_space=pltpu.VMEM)
    tile = jax.ShapeDtypeStruct((SIDE, SIDE), jnp.bfloat16)
    return pl.pallas_call(
        step_kernel,
        name="step",
        out_shape=(jax.ShapeDtypeStruct((16, SIDE, SIDE), jnp.bfloat16), tile, tile),
        in_specs=[pl.BlockSpec(memory_space=pltpu.HBM)] * 8,
        out_specs=(vmem, vmem, vmem),
        scratch_shapes=[
            pltpu.SMEM((16, 16), jnp.int32),
            pltpu.SMEM((4, 16), jnp.int32),
            pltpu.VMEM((128, 256), jnp.bfloat16),
            pltpu.VMEM((128, 1024), jnp.bfloat16),
            pltpu.VMEM((SIDE, SIDE), jnp.float32),
            pltpu.VMEM((SIDE, SIDE), jnp.float32),
            pltpu.VMEM((SIDE, SIDE), jnp.bfloat16),
            pltpu.VMEM((SIDE, SIDE), jnp.bfloat16),
            dma((8,)),
            pltpu.VMEM((NZ, 256, SIDE), jnp.bfloat16),
            pltpu.VMEM((4, 2, 2, NX, FEAT, 256), jnp.bfloat16),
            pltpu.VMEM((256, 128), jnp.bfloat16),
            pltpu.VMEM((8, 2, FEAT, 256), jnp.float32),
            pltpu.SMEM((16,), jnp.int32),
            pltpu.VMEM((16, FEAT, 256), jnp.bfloat16),
            pltpu.VMEM((SIDE, SIDE), jnp.bfloat16),
            dma((2,)), dma((2,)), dma((2, 4, 2)), dma((2, 4, 2)), dma((4,)), dma((NZ,)), dma((2, 2, 4)), dma((2, 2, 4)),
            dma((2,)), dma((2,)), dma((16,)), dma((16,)), dma,
            dma((2, 4)), dma((2, 4)), dma((2, 4, 2)), dma((2, 4, 2)), dma((9,)), dma((9,)), dma, dma,
        ],
        compiler_params=pltpu.CompilerParams(collective_id=1, has_side_effects=True, vmem_limit_bytes=VMEM_LIMIT),
        cost_estimate=pl.CostEstimate(flops=2 * 512**3 * 24, bytes_accessed=20 << 20, transcendentals=0),
    )(*(
        pltpu.with_memory_space_constraint(x, pltpu.HBM)
        for x in (block_slot, refresh_list.T, activations, out_grad, left_factor, right_factor, left_root, right_root)
    ))


def arrange_kernel(slots_hbm, every, left, right, out_hbm, nl_hbm, nr_hbm, slots_ref, sem):
    mp = lax.axis_index("mp")
    load = pltpu.make_async_copy(slots_hbm, slots_ref, sem.at[16])
    load.start()
    copies = [
        pltpu.make_async_copy(left, nl_hbm, sem.at[17]),
        pltpu.make_async_copy(right, nr_hbm, sem.at[18]),
    ]
    for copy in copies:
        copy.start()
    load.wait()
    for b in range(16):
        copy = pltpu.make_async_copy(
            every.at[slots_ref[mp, b]],
            out_hbm.at[pl.ds((b // 2) * SIDE, SIDE), pl.ds((b % 2) * SIDE, SIDE)],
            sem.at[b],
        )
        copy.start()
        copies.append(copy)
    for copy in copies:
        copy.wait()


def arrange(block_slot, every, left, right):
    hbm = pl.BlockSpec(memory_space=pltpu.HBM)
    vmem = pl.BlockSpec(memory_space=pltpu.VMEM)
    tile = jax.ShapeDtypeStruct((SIDE, SIDE), jnp.bfloat16)
    return pl.pallas_call(
        arrange_kernel,
        name="arrange",
        in_specs=[hbm, vmem, vmem, vmem],
        out_specs=(hbm, hbm, hbm),
        out_shape=(jax.ShapeDtypeStruct((8 * SIDE, 2 * SIDE), jnp.bfloat16), tile, tile),
        scratch_shapes=[pltpu.SMEM((16, 16), jnp.int32), pltpu.SemaphoreType.DMA((19,))],
        compiler_params=pltpu.CompilerParams(vmem_limit_bytes=VMEM_LIMIT),
        cost_estimate=pl.CostEstimate(flops=0, bytes_accessed=16 << 20, transcendentals=0),
    )(pltpu.with_memory_space_constraint(block_slot, pltpu.HBM), every, left, right)


def body(
    activations,
    out_grad,
    block_slot,
    refresh_list,
    left_factor,
    right_factor,
    left_root,
    right_root,
):
    every, new_left, new_right = step(
        block_slot, refresh_list, activations, out_grad,
        left_factor[0, 0], right_factor[0, 0], left_root[0, 0], right_root[0, 0],
    )
    direction, new_left, new_right = arrange(block_slot, every, new_left, new_right)
    return (direction, new_left[None, None], new_right[None, None])


def solution(mesh):
    in_specs = (
        P("dp", "mp"),
        P("dp", "mp"),
        P(),
        P(),
        P("dp", "mp", None, None),
        P("dp", "mp", None, None),
        P("dp", "mp", None, None),
        P("dp", "mp", None, None),
    )
    out_specs = (P(None, "mp"), P("dp", "mp", None, None), P("dp", "mp", None, None))
    return jax.shard_map(body, mesh=mesh, in_specs=in_specs, out_specs=out_specs, check_vma=False)
```

```python
import jax
import jax.numpy as jnp
from jax import lax
from jax.experimental import pallas as pl
from jax.experimental.pallas import tpu as pltpu
from jax.sharding import PartitionSpec as P

NZ, NX, NY = 8, 4, 4
SIDE = 512
FEAT = 64
A_ROWS = 288
HALF = A_ROWS // 2
MESH = pl.DeviceIdType.MESH
VMEM_LIMIT = 40 * 1024 * 1024


def place():
    dp, mp = lax.axis_index("dp"), lax.axis_index("mp")
    return dp // 2, dp % 2, mp // 8, (mp // 2) % 4, mp % 2


def device(z, h, l, x, k):
    return (2 * z + h, 8 * l + 2 * x + k)


def inverse_roots(statistics):
    shape = statistics[0].shape
    rows = lax.broadcasted_iota(jnp.int32, shape, 0)
    cols = lax.broadcasted_iota(jnp.int32, shape, 1)
    identity = jnp.where(rows == cols, 1.0, 0.0).astype(jnp.float32)

    def dot(left, right):
        return jnp.dot(left, right, preferred_element_type=jnp.float32)

    def parts(value, wide):
        high = value.astype(jnp.bfloat16)
        return (high, (value - high.astype(jnp.float32)).astype(jnp.bfloat16)) if wide else (high,)

    def product(left, right):
        total = dot(left[0], right[0])
        if len(left) == 2:
            total += dot(left[0], right[1]) + dot(left[1], right[0])
        return total

    def next_dev(dev, wide):
        narrow = [parts(e, wide) for e in dev]
        d = [2.5 * e - product(n, n) for e, n in zip(dev, narrow)]
        d_n = [parts(x, wide) for x in d]
        h = [parts(3.125 * x - product(n, n), wide) for x, n in zip(d, d_n)]
        return [2.44140625 * e - product(x, n) for e, x, n in zip(dev, h, narrow)]

    def plain(left, right):
        return dot(left.astype(jnp.bfloat16), right.astype(jnp.bfloat16))

    scaling = [2.5 / jnp.sqrt(jnp.sum(a * a)) for a in statistics]
    first = [a * (0.25 * c) for a, c in zip(statistics, scaling)]
    second = next_dev(first, True)
    third = next_dev(second, False)
    pair = [1.25 * (e + f) - plain(e, f) for e, f in zip(first, second)]
    result = [1.953125 * identity - 1.25 * p - 1.5625 * e + plain(p, e) for p, e in zip(pair, third)]
    return [(x * jnp.sqrt(jnp.sqrt(c))).astype(jnp.bfloat16) for x, c in zip(result, scaling)]


def step_kernel(
    slots_hbm, refresh_hbm, act_hbm, out_hbm, lf_hbm, rf_hbm, lr_hbm, rr_hbm, every, nl_ref, nr_ref,
    slots_ref, refresh_ref, act_ref, out_ref, lf_ref, rf_ref, lr_ref, rr_ref, load_s, cot, act, flipped, total, table, outgoing, tile,
    swap_s, swap_r, ring_s, ring_r, turn_s, turn_r, plane_s, plane_r,
    pass_s, pass_r, give_s, give_r, local_s, z_s, z_r, zb_s, zb_r, y_s, y_r, yb_s, yb_r,
):
    z, h, l, x, k = place()
    dp, mp = lax.axis_index("dp"), lax.axis_index("mp")
    y = 2 * h + l
    up, down = (z + 1) % NZ, (z + NZ - 1) % NZ

    loads = [
        pltpu.make_async_copy(src, dst, load_s.at[i])
        for i, (src, dst) in enumerate(
            (
                (act_hbm, act_ref), (out_hbm, out_ref), (slots_hbm, slots_ref), (refresh_hbm, refresh_ref),
                (lf_hbm, lf_ref), (rf_hbm, rf_ref), (lr_hbm, lr_ref), (rr_hbm, rr_ref),
            )
        )
    ]
    loads[1].start()
    barrier = pltpu.get_barrier_semaphore()

    def x_peer(step):
        return device(z, h, l, (x + step) % NX, k)

    def y_peer(step):
        there = (y + step) % NY
        return device(z, there // 2, there % 2, x, k)

    def greet(target):
        pl.semaphore_signal(barrier, inc=1, device_id=target, device_id_type=MESH)

    for i in range(4):
        source = 2 * i + k

        @pl.when(jnp.logical_not(jnp.logical_and(source == z, z // 4 == k)))
        def _():
            greet(device(source, h, l, x, z // 4))

    greet(device(up, h, l, x, k))
    greet(device(down, h, l, x, k))
    for step in range(1, 4):
        greet(x_peer(step))
        greet(y_peer(step))
    for copy in (loads[0], *loads[2:]):
        copy.start()

    loads[1].wait()
    for c in range(2):
        cot[z, pl.ds(h * 128, 128), c * 256 : c * 256 + 256] = out_ref[
            :, pl.ds(pl.multiple_of(c * 512 + 256 * h, 256), 256)
        ]
    pl.semaphore_wait(barrier, 12 - jnp.where(jnp.logical_and(z // 4 == k, z % 2 == k), 1, 0))

    def send(src, dst, ssem, rsem, target):
        copy = pltpu.make_async_remote_copy(
            src_ref=src, dst_ref=dst, send_sem=ssem, recv_sem=rsem, device_id=target, device_id_type=MESH
        )
        copy.start()
        return copy

    pending = []

    for c in range(2):
        pending.append(
            send(
                out_ref.at[:, pl.ds(pl.multiple_of(c * 512 + 256 * (1 - h), 256), 256)],
                cot.at[z, pl.ds(pl.multiple_of(h * 128, 128), 128), pl.ds(c * 256, 256)],
                swap_s.at[c], swap_r.at[c], (2 * z + 1 - h, mp),
            )
        )

    def unit(source, u):
        return cot.at[source, pl.ds(pl.multiple_of(u * 128, 128), 128), :]

    def ring(direction, step, u):
        source = (z + NZ - step) % NZ if direction == 0 else (z + step) % NZ
        target = up if direction == 0 else down
        view = unit(source, u)
        pending.append(
            send(view, view, ring_s.at[direction, step, u], ring_r.at[direction, step, u], (2 * target + h, mp))
        )

    def ring_wait(direction, step, u):
        source = (z + NZ - step) % NZ if direction == 0 else (z + step) % NZ
        view = unit(source, u)
        pltpu.make_async_remote_copy(
            src_ref=view, dst_ref=view, send_sem=ring_s.at[direction, step - 1, u],
            recv_sem=ring_r.at[direction, step - 1, u], device_id=(dp, mp), device_id_type=MESH,
        ).wait_recv()

    ring(0, 0, h)
    ring(1, 0, h)


    loads[0].wait()
    flipped[...] = act_ref[...].astype(jnp.float32).T.astype(jnp.bfloat16)

    def turn_view(source):
        return act.at[source // 2, source % 2, l, x, :, pl.ds(pl.multiple_of(h * 128, 128), 128)]

    for j in range(4):
        target = 4 * k + j
        here = jnp.logical_and(target == z, z % 2 == k)
        src = flipped.at[j * FEAT : (j + 1) * FEAT, :]

        @pl.when(jnp.logical_not(here))
        def _():
            send(src, turn_view(z), turn_s.at[j], turn_r.at[z], device(target, h, l, x, z % 2))

        @pl.when(here)
        def _():
            pltpu.make_async_copy(src, turn_view(z), turn_r.at[z]).start()

    for c in range(2):
        view = cot.at[z, pl.ds(pl.multiple_of((1 - h) * 128, 128), 128), pl.ds(c * 256, 256)]
        pltpu.make_async_copy(view, view, swap_r.at[c]).wait()
    ring(0, 0, 1 - h)
    ring(1, 0, 1 - h)

    for i in range(4):
        source = 2 * i + k
        view = turn_view(source)
        pltpu.make_async_copy(view, view, turn_r.at[source]).wait()

    def tokens(half):
        return pl.ds(pl.multiple_of(half * 128, 128), 128)

    def first_view(part, col, row):
        return act.at[2 * part : 2 * part + 2, k, row % 2, col, :, tokens(row // 2)]

    def second_view(part, index):
        if part == 0:
            return act.at[0:2, k, index % 2, :, :, tokens(index // 2)]
        return act.at[2:4, k, :, index]

    def peer(axis, step):
        return x_peer(step) if axis == 0 else y_peer(step)

    def back(axis, step):
        return (x + NX - step) % NX if axis == 0 else (y + NY - step) % NY

    for step in (1, 2, 3):
        for part in (0, 1):
            view = first_view(part, x, y)
            pending.append(send(view, view, plane_s.at[0, part, step], plane_r.at[0, part, step], peer(part, step)))

    def advance(step):
        for u in (h, 1 - h):
            for direction in (0, 1):
                ring_wait(direction, step, u)
                ring(direction, step, u)

    advance(1)
    for part in (0, 1):
        for step in (1, 2, 3):
            view = first_view(0, back(0, step), y) if part == 0 else first_view(1, x, back(1, step))
            pltpu.make_async_copy(view, view, plane_r.at[0, part, step]).wait()
        view = second_view(part, y if part == 0 else x)
        for step in (1, 2, 3):
            pending.append(
                send(view, view, plane_s.at[1, part, step], plane_r.at[1, part, step], peer(1 - part, step))
            )
    advance(2)

    for part in (0, 1):
        for step in (1, 2, 3):
            view = second_view(part, back(1 - part, step))
            pltpu.make_async_copy(view, view, plane_r.at[1, part, step]).wait()
        view = act.at[2 * part : 2 * part + 2, k]
        pending.append(send(view, view, pass_s.at[part], pass_r.at[part], device(z, h, l, x, 1 - k)))

    def held(slot):
        found = jnp.int32(0)
        for b in range(16):
            found = jnp.maximum(found, jnp.where(slots_ref[mp, b] == slot, b, 0))
        return found

    loads[2].wait()
    loads[3].wait()
    for slot in range(16):
        table[slot] = held(slot)

    for u in (h, 1 - h):
        for direction in (0, 1):
            ring_wait(direction, 3, u)
    ring(0, 3, 0)
    ring(1, 3, 1)

    for part in (0, 1):
        view = act.at[2 * part : 2 * part + 2, 1 - k]
        pltpu.make_async_copy(view, view, pass_r.at[part]).wait()

    def product(source):
        return jnp.dot(
            act[source // 2, source % 2].reshape(8 * FEAT, 256), cot[source], preferred_element_type=jnp.float32
        )

    def add(value):
        for c in range(2):
            total[:, c] += value[:, c * 256 : (c + 1) * 256].reshape(8, FEAT, 256)

    total[...] = jnp.zeros_like(total)
    add(product(z))

    @pl.loop(1, 4)
    def _(step):
        add(product((z + step) % NZ) + product((z + NZ - step) % NZ))

    ring_wait(0, 4, 0)
    ring_wait(1, 4, 1)
    add(product((z + 4) % NZ))

    def piece(slot):
        block = table[slot]
        return total[block // 2, block % 2].astype(jnp.bfloat16)

    def spot(slot):
        return tile.at[
            pl.ds(pl.multiple_of((slot // 2) * FEAT, FEAT), FEAT), pl.ds(pl.multiple_of((slot % 2) * 256, 256), 256)
        ]

    for dz in (4, 3, 5, 2, 6, 1, 7, 0):
        for dh in (0, 1):
            if (dz, dh) != (0, 0):
                slot = 2 * ((z + dz) % NZ) + (h + dh) % 2
                outgoing[slot] = piece(slot)
                send(outgoing.at[slot], spot(dp), give_s.at[slot], give_r.at[dp], (slot, mp))

    outgoing[dp] = piece(dp)
    own = pltpu.make_async_copy(outgoing.at[dp], spot(dp), local_s)
    own.start()
    own.wait()

    @pl.loop(1, 16)
    def _(step):
        slot = (dp + step) % 16
        view = spot(slot)
        pltpu.make_async_copy(view, view, give_r.at[slot]).wait()

    for copy in loads[4:]:
        copy.wait()
    mine = table[dp]
    hits = jnp.int32(0)
    for j in range(4):
        hits += jnp.where(refresh_ref[j, mp] == mine, 1, 0)
    chosen = jnp.broadcast_to(hits > 0, (SIDE, SIDE))
    grad = tile[...]
    left = lax.dot_general(grad, grad, (((1,), (1,)), ((), ())), preferred_element_type=jnp.float32)
    right = lax.dot_general(grad, grad, (((0,), (0,)), ((), ())), preferred_element_type=jnp.float32)
    lroot, rroot = inverse_roots((0.9 * lf_ref[...] + left, 0.9 * rf_ref[...] + right))
    nl_ref[...] = jnp.where(chosen, lroot, lr_ref[...])
    nr_ref[...] = jnp.where(chosen, rroot, rr_ref[...])
    mixed = jnp.dot(nl_ref[...], grad, preferred_element_type=jnp.float32).astype(jnp.bfloat16)
    precond = jnp.dot(mixed, nr_ref[...], preferred_element_type=jnp.float32)
    wide = grad.astype(jnp.float32)
    ratio = jnp.sqrt((jnp.sum(wide * wide) + 1e-06) / (jnp.sum(precond * precond) + 1e-06))
    every[dp] = (precond * ratio).astype(jnp.bfloat16)

    ends = ((2 * up + h, mp), (2 * down + h, mp))
    partner = (2 * z + 1 - h, mp)

    def arrived(view, sem):
        pltpu.make_async_copy(view, view, sem).wait()

    def source(direction, step):
        return (z + NZ - step) % NZ if direction == 0 else (z + step) % NZ

    def a_rows(direction, step):
        if step < 3:
            return pl.ds(0, A_ROWS)
        return pl.ds(direction * HALF, HALF)

    def post(src, dst, ssem, rsem, target):
        pending.append(send(src, dst, ssem, rsem, target))

    def a_view(slot, rows):
        return every.at[slot, rows, :]

    def b_view(slot):
        return every.at[slot, pl.ds(A_ROWS, SIDE - A_ROWS), :]

    def z_a(direction, step):
        rows = a_rows(direction, step)
        dst = a_view(2 * source(direction, step) + h, rows)
        src = dst
        post(src, dst, z_s.at[direction, step], z_r.at[direction, step], ends[direction])

    def z_b(direction, step, u):
        dst = b_view(2 * source(direction, step) + u)
        src = dst
        post(src, dst, zb_s.at[direction, step, u], zb_r.at[direction, step, u], ends[direction])

    def y_a(index, slot, rows):
        dst = a_view(slot, rows)
        post(dst, dst, y_s.at[index], y_r.at[index], partner)

    full = pl.ds(0, A_ROWS)
    z_a(0, 0)
    z_a(1, 0)
    post(b_view(dp), b_view(dp), yb_s, yb_r, partner)
    y_a(0, dp, full)
    z_b(0, 0, h)
    z_b(1, 0, h)
    arrived(b_view(2 * z + 1 - h), yb_r)
    z_b(0, 0, 1 - h)
    z_b(1, 0, 1 - h)

    for step in (1, 2, 3):
        for direction in (0, 1):
            slot = 2 * source(direction, step) + h
            arrived(a_view(slot, full), z_r.at[direction, step - 1])
            z_a(direction, step)
            y_a(1 + 3 * direction + step - 1, slot, full)
        for u in (h, 1 - h):
            for direction in (0, 1):
                arrived(b_view(2 * source(direction, step) + u), zb_r.at[direction, step - 1, u])
                if step < 3:
                    z_b(direction, step, u)
        if step == 3:
            z_b(0, 3, 0)
            z_b(1, 3, 1)
    for direction in (0, 1):
        rows = a_rows(direction, 3)
        slot = 2 * source(direction, 4) + h
        arrived(a_view(slot, rows), z_r.at[direction, 3])
        y_a(7 + direction, slot, rows)
    arrived(b_view(2 * source(0, 4)), zb_r.at[0, 3, 0])
    arrived(b_view(2 * source(1, 4) + 1), zb_r.at[1, 3, 1])

    other = 1 - h
    arrived(a_view(2 * z + other, full), y_r.at[0])
    for direction in (0, 1):
        for step in (1, 2, 3):
            arrived(a_view(2 * source(direction, step) + other, full), y_r.at[1 + 3 * direction + step - 1])
    for direction in (0, 1):
        arrived(a_view(2 * source(direction, 4) + other, a_rows(direction, 3)), y_r.at[7 + direction])

    for copy in pending:
        copy.wait_send()

    @pl.loop(1, 16)
    def _(step):
        slot = (dp + step) % 16
        pltpu.make_async_copy(outgoing.at[slot], outgoing.at[slot], give_s.at[slot]).wait()

    for j in range(4):
        here = jnp.logical_and(4 * k + j == z, z % 2 == k)
        src = flipped.at[j * FEAT : (j + 1) * FEAT, :]

        @pl.when(jnp.logical_not(here))
        def _():
            pltpu.make_async_copy(src, src, turn_s.at[j]).wait()


def step(block_slot, refresh_list, activations, out_grad, left_factor, right_factor, left_root, right_root):
    dma = pltpu.SemaphoreType.DMA
    vmem = pl.BlockSpec(memory_space=pltpu.VMEM)
    tile = jax.ShapeDtypeStruct((SIDE, SIDE), jnp.bfloat16)
    return pl.pallas_call(
        step_kernel,
        name="step",
        out_shape=(jax.ShapeDtypeStruct((16, SIDE, SIDE), jnp.bfloat16), tile, tile),
        in_specs=[pl.BlockSpec(memory_space=pltpu.HBM)] * 8,
        out_specs=(vmem, vmem, vmem),
        scratch_shapes=[
            pltpu.SMEM((16, 16), jnp.int32),
            pltpu.SMEM((4, 16), jnp.int32),
            pltpu.VMEM((128, 256), jnp.bfloat16),
            pltpu.VMEM((128, 1024), jnp.bfloat16),
            pltpu.VMEM((SIDE, SIDE), jnp.float32),
            pltpu.VMEM((SIDE, SIDE), jnp.float32),
            pltpu.VMEM((SIDE, SIDE), jnp.bfloat16),
            pltpu.VMEM((SIDE, SIDE), jnp.bfloat16),
            dma((8,)),
            pltpu.VMEM((NZ, 256, SIDE), jnp.bfloat16),
            pltpu.VMEM((4, 2, 2, NX, FEAT, 256), jnp.bfloat16),
            pltpu.VMEM((256, 128), jnp.bfloat16),
            pltpu.VMEM((8, 2, FEAT, 256), jnp.float32),
            pltpu.SMEM((16,), jnp.int32),
            pltpu.VMEM((16, FEAT, 256), jnp.bfloat16),
            pltpu.VMEM((SIDE, SIDE), jnp.bfloat16),
            dma((2,)), dma((2,)), dma((2, 4, 2)), dma((2, 4, 2)), dma((4,)), dma((NZ,)), dma((2, 2, 4)), dma((2, 2, 4)),
            dma((2,)), dma((2,)), dma((16,)), dma((16,)), dma,
            dma((2, 4)), dma((2, 4)), dma((2, 4, 2)), dma((2, 4, 2)), dma((9,)), dma((9,)), dma, dma,
        ],
        compiler_params=pltpu.CompilerParams(collective_id=1, has_side_effects=True, vmem_limit_bytes=VMEM_LIMIT),
        cost_estimate=pl.CostEstimate(flops=2 * 512**3 * 24, bytes_accessed=20 << 20, transcendentals=0),
    )(*(
        pltpu.with_memory_space_constraint(x, pltpu.HBM)
        for x in (block_slot, refresh_list.T, activations, out_grad, left_factor, right_factor, left_root, right_root)
    ))


def arrange_kernel(slots_hbm, every, left, right, out_hbm, nl_hbm, nr_hbm, slots_ref, sem):
    mp = lax.axis_index("mp")
    load = pltpu.make_async_copy(slots_hbm, slots_ref, sem.at[16])
    load.start()
    copies = [
        pltpu.make_async_copy(left, nl_hbm, sem.at[17]),
        pltpu.make_async_copy(right, nr_hbm, sem.at[18]),
    ]
    for copy in copies:
        copy.start()
    load.wait()
    for b in range(16):
        copy = pltpu.make_async_copy(
            every.at[slots_ref[mp, b]],
            out_hbm.at[pl.ds((b // 2) * SIDE, SIDE), pl.ds((b % 2) * SIDE, SIDE)],
            sem.at[b],
        )
        copy.start()
        copies.append(copy)
    for copy in copies:
        copy.wait()


def arrange(block_slot, every, left, right):
    hbm = pl.BlockSpec(memory_space=pltpu.HBM)
    vmem = pl.BlockSpec(memory_space=pltpu.VMEM)
    tile = jax.ShapeDtypeStruct((SIDE, SIDE), jnp.bfloat16)
    return pl.pallas_call(
        arrange_kernel,
        name="arrange",
        in_specs=[hbm, vmem, vmem, vmem],
        out_specs=(hbm, hbm, hbm),
        out_shape=(jax.ShapeDtypeStruct((8 * SIDE, 2 * SIDE), jnp.bfloat16), tile, tile),
        scratch_shapes=[pltpu.SMEM((16, 16), jnp.int32), pltpu.SemaphoreType.DMA((19,))],
        compiler_params=pltpu.CompilerParams(vmem_limit_bytes=VMEM_LIMIT),
        cost_estimate=pl.CostEstimate(flops=0, bytes_accessed=16 << 20, transcendentals=0),
    )(pltpu.with_memory_space_constraint(block_slot, pltpu.HBM), every, left, right)


def body(
    activations,
    out_grad,
    block_slot,
    refresh_list,
    left_factor,
    right_factor,
    left_root,
    right_root,
):
    every, new_left, new_right = step(
        block_slot, refresh_list, activations, out_grad,
        left_factor[0, 0], right_factor[0, 0], left_root[0, 0], right_root[0, 0],
    )
    direction, new_left, new_right = arrange(block_slot, every, new_left, new_right)
    return (direction, new_left[None, None], new_right[None, None])


def solution(mesh):
    in_specs = (
        P("dp", "mp"),
        P("dp", "mp"),
        P(),
        P(),
        P("dp", "mp", None, None),
        P("dp", "mp", None, None),
        P("dp", "mp", None, None),
        P("dp", "mp", None, None),
    )
    out_specs = (P(None, "mp"), P("dp", "mp", None, None), P("dp", "mp", None, None))
    return jax.shard_map(body, mesh=mesh, in_specs=in_specs, out_specs=out_specs, check_vma=False)
```
